128 devices in a mesh: dp: 16 (over x, y), seq: 8 (over z, core).
Axes of the slice: x: 4, y: 4, z: 4, core: 2. Of those that a mesh axis runs over, the one named last changes fastest.
Arguments:
- queries: bfloat16 [16, 8, 384, 1024], P('dp', 'seq'), may hold values from -6 to 6
- keys: bfloat16 [16, 8, 384, 1024], P('dp', 'seq'), may hold values from -6 to 6
- values: bfloat16 [16, 8, 384, 1024], P('dp', 'seq'), may hold values from -6 to 6
- gates: bfloat16 [16, 8, 384, 1024], P('dp', 'seq'), may hold values from -6 to 6
- attended: bfloat16 [16, 8, 384, 1024], P('dp', 'seq')
- out_grad: bfloat16 [16, 8, 384, 1024], P('dp', 'seq'), may hold values from -6 to 6
- plan: int32 [16, 8, 16], P(None, 'seq'), may hold values from 1 to 24, 256 in all within a row
- hist_len: int32 [16], P('dp'), may hold values from 512 to 2048, as said below
- block_mask: int32 [16, 16, 16], P('dp'), may hold values 0 or 1
Outputs:
- query_grad: bfloat16 [16, 8, 384, 1024], P('dp', 'seq')
- key_grad: bfloat16 [16, 8, 384, 1024], P('dp', 'seq')
- value_grad: bfloat16 [16, 8, 384, 1024], P('dp', 'seq')
- gate_grad: bfloat16 [16, 8, 384, 1024], P('dp', 'seq')
The draws below stay inside these ranges and needn't reach their ends.
Inputs may be any that keep to these rules, and one draw needn't show every extreme that they name: For every history g and piece s, plan[g, s, :] sums to 256; some entry of each such row equals 24. `hist_len`: some history has exactly 2048 events.
All inputs are finite; a program needn't handle non-finite values. No bound on the sum of `block_mask` on one device may be relied on, other than what follows from the above.
Results may differ from the reference program's by a relative error of at most 0.0058.
Values may be sent and summed in bfloat16 or wider, within the bound.
A program may use at most 128 MiB of HBM per device.

```python
import math
import jax
import jax.numpy as jnp
import numpy as np
from jax import lax

D = 1024
HEADS = 8
DH = 128
ROWS = 256
BLOCK = 128
GROUPS = 16
PIECES = 8
SLOT = 24
CAP = 384
LEN = 2048
NBLK = 16


def draw_hist_len(key, part):
    first_key, second_key = jax.random.split(key)
    lengths = jax.random.randint(first_key, (GROUPS,), LEN // 4, LEN + 1)
    chosen = jax.random.randint(second_key, (), 0, GROUPS)
    return jnp.where(jnp.arange(GROUPS) == chosen, LEN, lengths).astype(jnp.int32)


def draw_attended(key, part):
    key_list = jax.random.split(key, 3)
    row_scale = jnp.exp(jax.random.uniform(key_list[1], (GROUPS, PIECES, CAP, 1), jnp.float32, 0.0, math.log(10.0)))
    col_scale = jnp.exp(jax.random.uniform(key_list[2], (D,), jnp.float32, 0.0, math.log(10.0)))
    base = jax.random.normal(key_list[0], (GROUPS, PIECES, CAP, D), jnp.float32)
    result = row_scale * col_scale * base
    return result.astype(jnp.bfloat16)


def plant(values, own_key, low, top_value):
    extent = values.shape
    index_at = [jax.random.randint(jax.random.fold_in(own_key, axis), (), 0, extent[axis]) for axis in range(len(extent))]
    values = values.at[tuple(index_at)].set(low)
    longest = extent.index(max(extent))
    index_at[longest] = (index_at[longest] + 1) % extent[longest]
    return values.at[tuple(index_at)].set(top_value)


def steps_of(rng, shape, shards, smallest, top_value):
    level = 1.0
    for axis_at, blocks in shards:
        draws = jax.random.uniform(jax.random.fold_in(jax.random.fold_in(rng, 6), axis_at), (blocks,), jnp.float32, smallest / len(shards), top_value / len(shards))
        level = level * jnp.repeat(jnp.exp(draws), shape[axis_at] // blocks).reshape((-1,) + (1,) * (len(shape) - 1 - axis_at))
    return level


def profile(count, total, reach, lean):
    loads = [(1 << 20) // math.isqrt(grade ** lean) + 1 for grade in range(2, count + 1)]
    surplus, holding = total - reach - (count - 1), [1] * (count - 1)
    while surplus > 0:
        candidates = [i for i in range(count - 1) if holding[i] < reach]
        whole, left = sum([loads[i] for i in candidates]), surplus
        for i in candidates:
            addition = min(reach - holding[i], max(1, left * loads[i] // whole), surplus)
            holding[i] = holding[i] + addition
            surplus = surplus - addition
    return np.array([reach] + holding)


def ragged_sizes(key, count, total, bound, slope):
    if count == 2:
        one = jax.random.randint(key, (), max(1, total - bound), min(bound, total - 1) + 1)
        return jnp.stack([one, total - one])
    sizes = jnp.asarray(profile(count, total, bound, slope), jnp.int32)
    twos = (count - 1) // 2
    giver, sink = sizes[1:1 + 2 * twos:2], sizes[2:2 + 2 * twos:2]
    slack = jnp.minimum(giver - 1, bound - sink)
    shifted = jax.random.randint(jax.random.fold_in(key, 1), (twos,), 0, 1 << 20) % (slack + 1)
    sizes = sizes.at[1:1 + 2 * twos:2].set(giver - shifted).at[2:2 + 2 * twos:2].set(sink + shifted)
    return sizes[jax.random.permutation(jax.random.fold_in(key, 2), count)]


def gaussian(own_key, extent, deviation, limit, cuts=(), kind=jnp.bfloat16):
    values = jax.random.normal(own_key, extent, jnp.float32) * deviation
    if len(cuts) > 0:
        values = steps_of(own_key, extent, cuts, -0.22, 0.18) * values
    return jnp.clip(values, min=-limit, max=limit).astype(kind)


def setup_inputs(seed: int = 0) -> dict:
    splits = jax.random.split(jax.random.key(seed), 10)
    queries = gaussian(splits[0], (GROUPS, PIECES, CAP, D), 1.0, 6.0, ((0, 16), (1, 8)))
    keys = gaussian(splits[1], (GROUPS, PIECES, CAP, D), 1.0, 6.0, ((0, 16), (1, 8)))
    values = gaussian(splits[2], (GROUPS, PIECES, CAP, D), 1.0, 6.0, ((0, 16), (1, 8)))
    gates = gaussian(splits[3], (GROUPS, PIECES, CAP, D), 1.0, 6.0, ((0, 16), (1, 8)))
    attended = draw_attended(jax.random.fold_in(splits[9], 71), 0)
    out_grad = gaussian(splits[5], (GROUPS, PIECES, CAP, D), 1.0, 6.0, ((0, 16), (1, 8)))
    plan = jax.vmap(lambda own: ragged_sizes(own, GROUPS, ROWS, SLOT, 2))(jax.random.split(splits[6], GROUPS * PIECES)).reshape((GROUPS, PIECES, GROUPS)).astype(jnp.int32)
    hist_len = draw_hist_len(jax.random.fold_in(splits[9], 71), 0)
    block_mask = plant((jax.random.randint(splits[8], (GROUPS, NBLK, NBLK), 0, 2) < 1).astype(jnp.int32), jax.random.fold_in(splits[8], 1), 0, 1)
    return {"queries": queries, "keys": keys, "values": values, "gates": gates, "attended": attended, "out_grad": out_grad, "plan": plan, "hist_len": hist_len, "block_mask": block_mask}


def layer_norm(inputs):
    center = inputs - lax.optimization_barrier(jnp.mean(inputs, axis=-1, keepdims=True))
    spread = lax.optimization_barrier(jnp.mean(center * center, axis=-1, keepdims=True))
    return center * lax.rsqrt(spread + 1e-05)

def head_terms(query_rows, key_rows, value_rows, grad_rows, live_weight):
    scale_qk = DH ** (-0.5)
    scores = jnp.dot(query_rows, key_rows.T, preferred_element_type=jnp.float32) * scale_qk
    sigmoid = jax.nn.sigmoid(scores)
    weight = (scores * sigmoid * live_weight).astype(jnp.bfloat16)
    products = jnp.dot(grad_rows, value_rows.T, preferred_element_type=jnp.float32)
    score_grad = (products * (sigmoid * (1.0 + scores * (1.0 - sigmoid))) * live_weight).astype(jnp.bfloat16)
    query_part = jnp.dot(score_grad, key_rows, preferred_element_type=jnp.float32) * scale_qk
    key_part = jnp.dot(score_grad.T, query_rows, preferred_element_type=jnp.float32) * scale_qk
    value_part = jnp.dot(weight.T, grad_rows, preferred_element_type=jnp.float32)
    return (query_part, key_part, value_part)

def group_terms(operands):
    query_all, key_all, value_all, grad_all, length, pattern = operands
    positions = jnp.arange(LEN, dtype=jnp.int32)
    block_of = positions // BLOCK
    onehot = (block_of[:, None] == jnp.arange(NBLK, dtype=jnp.int32)[None, :]).astype(jnp.float32)
    blocks = jnp.dot(jnp.dot(onehot, pattern.astype(jnp.float32), precision=lax.Precision.HIGHEST), onehot.T, precision=lax.Precision.HIGHEST)
    keep = (positions[None, :] <= positions[:, None]) & (positions[:, None] < length) & (positions[None, :] < length)
    keep = keep & ((blocks > 0.5) | (block_of[:, None] == block_of[None, :]))
    inverse = 1.0 / jnp.sqrt(length.astype(jnp.float32))
    live_weight = keep.astype(jnp.float32) * inverse

    def one_head(parts):
        return head_terms(parts[0], parts[1], parts[2], parts[3], live_weight)
    return lax.map(one_head, (query_all, key_all, value_all, grad_all))

def reference(queries, keys, values, gates, attended, out_grad, plan, hist_len, block_mask):
    normed, pullback = jax.vjp(layer_norm, attended.astype(jnp.float32))
    cotangent = out_grad.astype(jnp.float32) * gates.astype(jnp.float32)
    attn_grad = pullback(cotangent)[0].astype(jnp.bfloat16)
    plan = plan.astype(jnp.int32)
    cum_incl = jnp.cumsum(plan, axis=2).astype(jnp.int32)
    cum_excl = (cum_incl - plan).astype(jnp.int32)
    slot_ids = jnp.arange(SLOT, dtype=jnp.int32)
    incoming = jnp.transpose(plan, (2, 1, 0))
    valid = (slot_ids[None, None, None, :] < incoming[..., None]).reshape(GROUPS, PIECES, CAP)
    gate_grad = jnp.where(valid[..., None], out_grad.astype(jnp.float32) * normed, 0.0).astype(jnp.bfloat16)
    row_ids = jnp.arange(ROWS, dtype=jnp.int32)
    dest = lax.optimization_barrier(jnp.sum((cum_incl[:, :, None, :] <= row_ids[None, None, :, None]).astype(jnp.int32), axis=3)).astype(jnp.int32)
    begin = jnp.take_along_axis(cum_excl, dest, axis=2).astype(jnp.int32)
    group_ids = jnp.arange(GROUPS, dtype=jnp.int32)
    slot_index = (group_ids[:, None, None] * SLOT + row_ids[None, None, :] - begin).astype(jnp.int32)
    piece_index = jnp.arange(PIECES, dtype=jnp.int32)[None, :, None]

    def to_history(array):
        picked = array[dest, piece_index, slot_index]
        return picked.reshape(GROUPS, LEN, HEADS, DH).transpose(0, 2, 1, 3)
    histories = (to_history(queries), to_history(keys), to_history(values), to_history(attn_grad))
    grads = lax.map(group_terms, (histories[0], histories[1], histories[2], histories[3], hist_len.astype(jnp.int32), block_mask.astype(jnp.int32)))
    row_index = jnp.minimum(jnp.transpose(cum_excl, (2, 1, 0))[..., None] + slot_ids, ROWS - 1).astype(jnp.int32)
    group_index = group_ids[None, None, :, None]
    piece_back = jnp.arange(PIECES, dtype=jnp.int32)[None, :, None, None]

    def to_slots(history):
        rows_view = history.transpose(0, 2, 1, 3).reshape(GROUPS, PIECES, ROWS, D)
        picked = rows_view[group_index, piece_back, row_index].reshape(GROUPS, PIECES, CAP, D)
        return jnp.where(valid[..., None], picked, 0.0).astype(jnp.bfloat16)
    return (to_slots(grads[0]), to_slots(grads[1]), to_slots(grads[2]), gate_grad)
```

```python
import jax
import jax.numpy as jnp
from jax import lax
from jax.experimental import pallas as pl
from jax.experimental.pallas import tpu as pltpu
from jax.sharding import PartitionSpec as P

MESH = pl.DeviceIdType.MESH
F32 = jnp.float32
BF16 = jnp.bfloat16

DP = 16
SEQ = 8
SLOT = 24
CAP = 384
WIDTH = 1024
ROWS = 256
DH = 128
LEN = 2048
NBLK = 16
PACK = 2 * SLOT
HALF = 512
QUART = 256
SCALE = DH ** (-0.5)

Q, K, G, V = 0, 1, 2, 3
DV, DK, DQ = 0, 1, 2


def kernel(
    queries,
    keys,
    values,
    gates,
    attended,
    out_grad,
    plan,
    hist_len,
    block_mask,
    query_grad,
    key_grad,
    value_grad,
    gate_grad,
    stage,
    dsend,
    drecv,
    comp,
    hist,
    live,
    wt,
    dt,
    qacc,
    grads,
    gath,
    osend,
    orecv,
    ostage,
    gstage,
    place,
    spread,
    load_sem,
    store_sem,
    dsend_sem,
    drecv_sem,
    ssend_sem,
    srecv_sem,
    gsend_sem,
    grecv_sem,
    osend_sem,
    orecv_sem,
):
    dp = lax.axis_index("dp")
    sq = lax.axis_index("seq")
    row_x, row_y = dp // 4, lax.rem(dp, 4)
    zed, core = sq // 2, lax.rem(sq, 2)

    barrier = pltpu.get_barrier_semaphore()

    def greet_dp(k, carry):
        pl.semaphore_signal(
            barrier, inc=1, device_id=(lax.rem(dp + k, DP), sq), device_id_type=MESH
        )
        return carry

    def greet_seq(k, carry):
        pl.semaphore_signal(
            barrier, inc=1, device_id=(dp, lax.rem(sq + k, SEQ)), device_id_type=MESH
        )
        return carry

    lax.fori_loop(1, DP, greet_dp, 0)
    lax.fori_loop(1, SEQ, greet_seq, 0)

    sources = (queries, keys, attended, gates, out_grad, values)
    loads = [
        pltpu.make_async_copy(src.at[0, 0], stage.at[i], load_sem.at[i])
        for i, src in enumerate(sources)
    ]
    for load in loads:
        load.start()

    def remote(src, dst, send_sem, recv_sem, target):
        return pltpu.make_async_remote_copy(
            src_ref=src,
            dst_ref=dst,
            send_sem=send_sem,
            recv_sem=recv_sem,
            device_id=target,
            device_id_type=MESH,
        )

    def landed(ref, sem):
        remote(ref, ref, sem, sem, (dp, sq)).wait_recv()

    def left(ref, sem):
        remote(ref, ref, sem, sem, (dp, sq)).wait_send()

    def scatter_dp(src, dst, send_sems, recv_sems, chunk):
        def body(k, carry):
            off = k ^ 10
            peer = lax.rem(row_x + off // 4, 4) * 4 + lax.rem(row_y + lax.rem(off, 4), 4)

            @pl.when(k != 10)
            def _():
                remote(
                    src.at[chunk, peer],
                    dst.at[chunk, dp],
                    send_sems.at[chunk],
                    recv_sems.at[chunk],
                    (peer, sq),
                ).start()

            @pl.when(k == 10)
            def _():
                pltpu.make_async_copy(
                    src.at[chunk, dp], dst.at[chunk, dp], recv_sems.at[chunk]
                ).start()

            return carry

        lax.fori_loop(0, DP, body, 0)

    def pack_pair(block, array, pair):
        for half in range(2):
            for side in range(2):
                part = block[side * SLOT : (side + 1) * SLOT]
                at = half * HALF
                message = jnp.concatenate(
                    [part[:, at : at + QUART], part[:, at + QUART : at + HALF]], axis=0
                )
                dsend[2 * array + half, 2 * pair + side] = message.astype(BF16)

    def pack(array, slot):
        loads[slot].wait()

        def body(pair, carry):
            at = pl.multiple_of(pair * PACK, PACK)
            pack_pair(stage[slot, pl.ds(at, PACK), :].astype(F32), array, pair)
            return carry

        lax.fori_loop(0, DP // 2, body, 0)

    def send(array):
        for half in range(2):
            scatter_dp(dsend, drecv, dsend_sem, drecv_sem, 2 * array + half)

    pack(Q, 0)
    pl.semaphore_wait(barrier, DP - 1 + SEQ - 1)
    send(Q)
    pack(K, 1)
    send(K)

    for i in (2, 3, 4):
        loads[i].wait()
    row48 = lax.broadcasted_iota(jnp.int32, (PACK, 1), 0)

    def norm_body(pair, carry):
        at = pl.multiple_of(pair * PACK, PACK)
        inputs = stage[2, pl.ds(at, PACK), :].astype(F32)
        gate = stage[3, pl.ds(at, PACK), :].astype(F32)
        grad = stage[4, pl.ds(at, PACK), :].astype(F32)
        center = inputs - jnp.mean(inputs, axis=-1, keepdims=True)
        spread_ = jnp.mean(center * center, axis=-1, keepdims=True)
        inv = lax.rsqrt(spread_ + 1e-05)
        normed = center * inv
        first = plan[2 * pair, 0, dp]
        second = plan[2 * pair + 1, 0, dp]
        valid = row48 < jnp.where(row48 < SLOT, first, SLOT + second)
        gstage[pl.ds(at, PACK), :] = jnp.where(valid, grad * normed, 0.0).astype(BF16)
        cot = grad * gate
        mean_cot = jnp.mean(cot, axis=-1, keepdims=True)
        mean_dot = jnp.mean(cot * normed, axis=-1, keepdims=True)
        back = inv * (cot - mean_cot - normed * mean_dot)
        pack_pair(jnp.where(valid, back, 0.0), G, pair)
        return carry

    lax.fori_loop(0, DP // 2, norm_body, 0)
    send(G)
    gate_store = pltpu.make_async_copy(gstage, gate_grad.at[0, 0], store_sem.at[0])
    gate_store.start()
    pack(V, 5)
    send(V)

    lane768 = lax.broadcasted_iota(jnp.int32, (1, DP * PACK), 1)
    lane512 = lax.broadcasted_iota(jnp.int32, (1, 2 * ROWS), 1)
    side48 = jnp.where(row48 < SLOT, 0, 1)
    slot48 = row48 - side48 * SLOT

    def target_body(d, carry):
        begin, where_to = carry
        count = plan[dp, 0, d]
        i = lane768 - d * PACK
        side = jnp.where(i < SLOT, 0, 1)
        j = i - side * SLOT
        hit = (i >= 0) & (i < PACK) & (j < count)
        where_to = jnp.where(hit, side * ROWS + begin + j, where_to)
        at = jnp.where(slot48 < count, side48 * ROWS + begin + slot48, -1)
        spread[pl.ds(pl.multiple_of(d * PACK, PACK), PACK), :] = (
            jnp.where(lane512 == at, 1.0, 0.0).astype(BF16)
        )
        return begin + count, where_to

    _, where_to = lax.fori_loop(
        0, DP, target_body, (jnp.int32(0), jnp.full((1, DP * PACK), -1, jnp.int32))
    )

    def place_body(i, carry):
        at = pl.multiple_of(i * 64, 64)
        rows = lax.broadcasted_iota(jnp.int32, (64, 1), 0) + at
        place[pl.ds(at, 64), :] = jnp.where(rows == where_to, 1.0, 0.0).astype(BF16)
        return carry

    lax.fori_loop(0, 2 * ROWS // 64, place_body, 0)

    pattern = block_mask[0].astype(F32)
    block_row = lax.broadcasted_iota(jnp.int32, (NBLK, LEN), 0)
    pos = lax.broadcasted_iota(jnp.int32, (NBLK, LEN), 1)
    onehot = jnp.where(block_row == pos // DH, 1.0, 0.0)
    kept = lax.dot_general(
        pattern, onehot, (((0,), (0,)), ((), ())), preferred_element_type=F32
    )
    length = hist_len[0]
    total = jnp.full((NBLK, LEN), length, jnp.int32).astype(F32)
    inverse = 1.0 / jnp.sqrt(total)
    live[...] = jnp.where(
        ((kept > 0.5) | (onehot > 0.5)) & (pos < length), inverse, 0.0
    )

    def gather_rows(array):
        for half in range(2):
            chunk = 2 * array + half
            landed(drecv.at[chunk], drecv_sem.at[chunk])
            block = drecv[chunk].reshape(DP * PACK, QUART)
            comp[chunk] = jnp.dot(
                place[...], block, preferred_element_type=F32
            ).astype(BF16)
            for to in range(4):
                src = comp.at[
                    chunk, pl.ds(to // 2 * ROWS, ROWS), pl.ds(to % 2 * DH, DH)
                ]
                dst = hist.at[array, sq]
                peer = 2 * to + half

                @pl.when(sq != peer)
                def _():
                    remote(
                        src, dst, ssend_sem.at[array], srecv_sem.at[array], (dp, peer)
                    ).start()

                @pl.when(sq == peer)
                def _():
                    pltpu.make_async_copy(src, dst, srecv_sem.at[array]).start()

    def history(array):
        landed(hist.at[array], srecv_sem.at[array])

    nt = (((1,), (1,)), ((), ()))
    tn = (((0,), (0,)), ((), ()))

    def scores_tile(i, j, diagonal):
        at = pl.multiple_of(j * ROWS, ROWS)
        raw = lax.dot_general(hist[K, i], hist[Q, j], nt, preferred_element_type=F32)
        for part in range(2):
            rows = slice(part * DH, (part + 1) * DH)
            scores = raw[rows] * SCALE
            sig = 0.5 * jnp.tanh(scores * 0.5) + 0.5
            keep = live[pl.ds(2 * i + part, 1), pl.ds(at, ROWS)]
            if diagonal:
                s = lax.broadcasted_iota(jnp.int32, (DH, ROWS), 0) + part * DH
                t = lax.broadcasted_iota(jnp.int32, (DH, ROWS), 1)
                keep = jnp.where(s <= t, keep, 0.0)
            fac = sig * keep
            weight = scores * fac
            wt[i, pl.ds(part * DH, DH), pl.ds(at, ROWS)] = weight.astype(BF16)
            dt[i, pl.ds(part * DH, DH), pl.ds(at, ROWS)] = fac + weight * (1.0 - sig)

    def scores_strip(i, carry):
        scores_tile(i, i, True)

        def body(j, c):
            scores_tile(i, j, False)
            return c

        lax.fori_loop(i + 1, SEQ, body, 0)
        return carry

    def value_strip(i, carry):
        def body(j, acc):
            at = pl.multiple_of(j * ROWS, ROWS)
            return acc + jnp.dot(
                wt[i, :, pl.ds(at, ROWS)], hist[G, j], preferred_element_type=F32
            )

        acc = lax.fori_loop(i, SEQ, body, jnp.zeros((ROWS, DH), F32))
        grads[DV, i] = acc.astype(BF16)
        return carry

    def score_grad_strip(i, carry):
        def body(j, acc):
            at = pl.multiple_of(j * ROWS, ROWS)
            products = lax.dot_general(
                hist[V, i], hist[G, j], nt, preferred_element_type=F32
            )
            score_grad = (products * dt[i, :, pl.ds(at, ROWS)]).astype(BF16)
            qacc[j] += lax.dot_general(
                score_grad, hist[K, i], tn, preferred_element_type=F32
            )
            return acc + jnp.dot(score_grad, hist[Q, j], preferred_element_type=F32)

        acc = lax.fori_loop(i, SEQ, body, jnp.zeros((ROWS, DH), F32))
        grads[DK, i] = (acc * SCALE).astype(BF16)
        return carry

    def send_grads(out):
        def body(k, carry):
            peer = lax.rem(sq + 4 + k, SEQ)
            src = grads.at[out, peer]
            dst = gath.at[
                2 * out + core,
                zed // 2,
                :,
                pl.ds(pl.multiple_of(lax.rem(zed, 2) * DH, DH), DH),
            ]
            recv_sem = grecv_sem.at[2 * out + core]

            @pl.when(k != 4)
            def _():
                remote(src, dst, gsend_sem.at[out], recv_sem, (dp, peer)).start()

            @pl.when(k == 4)
            def _():
                pltpu.make_async_copy(src, dst, recv_sem).start()

            return carry

        lax.fori_loop(0, SEQ, body, 0)

    def return_rows(out):
        for half in range(2):
            chunk = 2 * out + half
            landed(gath.at[chunk], grecv_sem.at[chunk])
            block = gath[chunk].reshape(2 * ROWS, QUART)
            osend[chunk] = (
                jnp.dot(spread[...], block, preferred_element_type=F32)
                .astype(BF16)
                .reshape(DP, PACK, QUART)
            )
            scatter_dp(osend, orecv, osend_sem, orecv_sem, chunk)

    stores = []

    def finish(out, target):
        for half in range(2):
            chunk = 2 * out + half
            landed(orecv.at[chunk], orecv_sem.at[chunk])

            def body(pair, carry):
                at = pl.multiple_of(pair * PACK, PACK)
                one = orecv[chunk, 2 * pair].astype(F32)
                two = orecv[chunk, 2 * pair + 1].astype(F32)
                lo = jnp.concatenate([one[:SLOT], two[:SLOT]], axis=0)
                hi = jnp.concatenate([one[SLOT:], two[SLOT:]], axis=0)
                base = half * HALF
                ostage[out, pl.ds(at, PACK), base : base + QUART] = lo.astype(BF16)
                ostage[out, pl.ds(at, PACK), base + QUART : base + HALF] = hi.astype(BF16)
                return carry

            lax.fori_loop(0, DP // 2, body, 0)
            store = pltpu.make_async_copy(
                ostage.at[out, :, pl.ds(half * HALF, HALF)],
                target.at[0, 0, :, pl.ds(half * HALF, HALF)],
                store_sem.at[1 + chunk],
            )
            store.start()
            stores.append(store)

    qacc[...] = jnp.zeros_like(qacc)
    gather_rows(Q)
    gather_rows(K)
    history(Q)
    history(K)
    lax.fori_loop(0, 3, scores_strip, 0)
    gather_rows(G)
    lax.fori_loop(3, SEQ, scores_strip, 0)
    history(G)
    lax.fori_loop(0, SEQ, value_strip, 0)
    send_grads(DV)
    gather_rows(V)
    history(V)
    return_rows(DV)
    lax.fori_loop(0, SEQ, score_grad_strip, 0)
    send_grads(DK)
    grads[DQ] = (qacc[...] * SCALE).astype(BF16)
    send_grads(DQ)
    return_rows(DK)
    return_rows(DQ)
    finish(DV, value_grad)
    finish(DK, key_grad)
    finish(DQ, query_grad)

    for chunk in range(8):
        left(dsend.at[chunk, pl.ds(0, DP - 1)], dsend_sem.at[chunk])
    for array in range(4):
        left(hist.at[array, pl.ds(0, SEQ - 1)], ssend_sem.at[array])
    for out in range(3):
        left(grads.at[out, pl.ds(0, SEQ - 1)], gsend_sem.at[out])
    for chunk in range(6):
        left(osend.at[chunk, pl.ds(0, DP - 1)], osend_sem.at[chunk])
    gate_store.wait()
    for store in stores:
        store.wait()


def local(queries, keys, values, gates, attended, out_grad, plan, hist_len, block_mask):
    hbm = pl.BlockSpec(memory_space=pl.ANY)
    smem = pl.BlockSpec(memory_space=pltpu.SMEM)
    vmem = pl.BlockSpec(memory_space=pltpu.VMEM)
    out = jax.ShapeDtypeStruct((1, 1, CAP, WIDTH), BF16)
    dma = pltpu.SemaphoreType.DMA
    return pl.pallas_call(
        kernel,
        out_shape=(out,) * 4,
        in_specs=[hbm] * 6 + [smem, smem, vmem],
        out_specs=(hbm,) * 4,
        scratch_shapes=[
            pltpu.VMEM((6, CAP, WIDTH), BF16),
            pltpu.VMEM((8, DP, PACK, QUART), BF16),
            pltpu.VMEM((8, DP, PACK, QUART), BF16),
            pltpu.VMEM((8, 2 * ROWS, QUART), BF16),
            pltpu.VMEM((4, SEQ, ROWS, DH), BF16),
            pltpu.VMEM((NBLK, LEN), F32),
            pltpu.VMEM((SEQ, ROWS, LEN), BF16),
            pltpu.VMEM((SEQ, ROWS, LEN), F32),
            pltpu.VMEM((SEQ, ROWS, DH), F32),
            pltpu.VMEM((3, SEQ, ROWS, DH), BF16),
            pltpu.VMEM((6, 2, ROWS, QUART), BF16),
            pltpu.VMEM((6, DP, PACK, QUART), BF16),
            pltpu.VMEM((6, DP, PACK, QUART), BF16),
            pltpu.VMEM((3, CAP, WIDTH), BF16),
            pltpu.VMEM((CAP, WIDTH), BF16),
            pltpu.VMEM((2 * ROWS, DP * PACK), BF16),
            pltpu.VMEM((DP * PACK, 2 * ROWS), BF16),
            dma((6,)),
            dma((7,)),
            dma((8,)),
            dma((8,)),
            dma((4,)),
            dma((4,)),
            dma((3,)),
            dma((6,)),
            dma((6,)),
            dma((6,)),
        ],
        compiler_params=pltpu.CompilerParams(
            collective_id=1, has_side_effects=True, vmem_limit_bytes=60 * 2**20
        ),
    )(queries, keys, values, gates, attended, out_grad, plan, hist_len, block_mask)


def solution(mesh):
    rows = P("dp", "seq", None, None)
    return jax.shard_map(
        local,
        mesh=mesh,
        in_specs=(rows,) * 6 + (P(None, "seq", None), P("dp"), P("dp", None, None)),
        out_specs=(rows,) * 4,
        check_vma=False,
    )
```

```python
import jax
import jax.numpy as jnp
from jax import lax
from jax.experimental import pallas as pl
from jax.experimental.pallas import tpu as pltpu
from jax.sharding import PartitionSpec as P

MESH = pl.DeviceIdType.MESH
F32 = jnp.float32
BF16 = jnp.bfloat16

DP = 16
SEQ = 8
SLOT = 24
CAP = 384
WIDTH = 1024
ROWS = 256
DH = 128
LEN = 2048
NBLK = 16
PACK = 2 * SLOT
HALF = 512
QUART = 256
SCALE = DH ** (-0.5)
TILE = 512
TILES = LEN // TILE

Q, K, G, V = 0, 1, 2, 3
DV, DK, DQ = 0, 1, 2


def kernel(
    queries,
    keys,
    values,
    gates,
    attended,
    out_grad,
    plan,
    hist_len,
    block_mask,
    query_grad,
    key_grad,
    value_grad,
    gate_grad,
    stage,
    dsend,
    drecv,
    comp,
    hist,
    live,
    wt,
    dt,
    key_t,
    grads,
    gath,
    osend,
    orecv,
    ostage,
    gstage,
    place,
    spread,
    load_sem,
    store_sem,
    dsend_sem,
    drecv_sem,
    ssend_sem,
    srecv_sem,
    gsend_sem,
    grecv_sem,
    osend_sem,
    orecv_sem,
):
    dp = lax.axis_index("dp")
    sq = lax.axis_index("seq")
    row_x, row_y = dp // 4, lax.rem(dp, 4)
    zed, core = sq // 2, lax.rem(sq, 2)

    barrier = pltpu.get_barrier_semaphore()

    def greet_dp(k, carry):
        pl.semaphore_signal(
            barrier, inc=1, device_id=(lax.rem(dp + k, DP), sq), device_id_type=MESH
        )
        return carry

    def greet_seq(k, carry):
        pl.semaphore_signal(
            barrier, inc=1, device_id=(dp, lax.rem(sq + k, SEQ)), device_id_type=MESH
        )
        return carry

    lax.fori_loop(1, DP, greet_dp, 0)
    lax.fori_loop(1, SEQ, greet_seq, 0)

    sources = (queries, keys, attended, gates, out_grad, values)
    loads = [
        pltpu.make_async_copy(src.at[0, 0], stage.at[i], load_sem.at[i])
        for i, src in enumerate(sources)
    ]
    for load in loads:
        load.start()

    def remote(src, dst, send_sem, recv_sem, target):
        return pltpu.make_async_remote_copy(
            src_ref=src,
            dst_ref=dst,
            send_sem=send_sem,
            recv_sem=recv_sem,
            device_id=target,
            device_id_type=MESH,
        )

    def landed(ref, sem):
        remote(ref, ref, sem, sem, (dp, sq)).wait_recv()

    def left(ref, sem):
        remote(ref, ref, sem, sem, (dp, sq)).wait_send()

    def scatter_dp(src, dst, send_sems, recv_sems, chunk):
        def body(k, carry):
            off = k ^ 10
            peer = lax.rem(row_x + off // 4, 4) * 4 + lax.rem(row_y + lax.rem(off, 4), 4)

            @pl.when(k != 10)
            def _():
                remote(
                    src.at[chunk, peer],
                    dst.at[chunk, dp],
                    send_sems.at[chunk],
                    recv_sems.at[chunk],
                    (peer, sq),
                ).start()

            @pl.when(k == 10)
            def _():
                pltpu.make_async_copy(
                    src.at[chunk, dp], dst.at[chunk, dp], recv_sems.at[chunk]
                ).start()

            return carry

        lax.fori_loop(0, DP, body, 0)

    def pack_pair(block, array, pair):
        for half in range(2):
            for side in range(2):
                part = block[side * SLOT : (side + 1) * SLOT]
                at = half * HALF
                message = jnp.concatenate(
                    [part[:, at : at + QUART], part[:, at + QUART : at + HALF]], axis=0
                )
                dsend[2 * array + half, 2 * pair + side] = message.astype(BF16)

    def pack(array, slot):
        loads[slot].wait()

        def body(pair, carry):
            at = pl.multiple_of(pair * PACK, PACK)
            pack_pair(stage[slot, pl.ds(at, PACK), :].astype(F32), array, pair)
            return carry

        lax.fori_loop(0, DP // 2, body, 0)

    def send(array):
        for half in range(2):
            scatter_dp(dsend, drecv, dsend_sem, drecv_sem, 2 * array + half)

    pack(Q, 0)
    pl.semaphore_wait(barrier, DP - 1 + SEQ - 1)
    send(Q)
    pack(K, 1)
    send(K)

    for i in (2, 3, 4):
        loads[i].wait()
    row48 = lax.broadcasted_iota(jnp.int32, (PACK, 1), 0)

    def norm_body(pair, carry):
        at = pl.multiple_of(pair * PACK, PACK)
        inputs = stage[2, pl.ds(at, PACK), :].astype(F32)
        gate = stage[3, pl.ds(at, PACK), :].astype(F32)
        grad = stage[4, pl.ds(at, PACK), :].astype(F32)
        center = inputs - jnp.mean(inputs, axis=-1, keepdims=True)
        spread_ = jnp.mean(center * center, axis=-1, keepdims=True)
        inv = lax.rsqrt(spread_ + 1e-05)
        normed = center * inv
        first = plan[2 * pair, 0, dp]
        second = plan[2 * pair + 1, 0, dp]
        valid = row48 < jnp.where(row48 < SLOT, first, SLOT + second)
        gstage[pl.ds(at, PACK), :] = jnp.where(valid, grad * normed, 0.0).astype(BF16)
        cot = grad * gate
        mean_cot = jnp.mean(cot, axis=-1, keepdims=True)
        mean_dot = jnp.mean(cot * normed, axis=-1, keepdims=True)
        back = inv * (cot - mean_cot - normed * mean_dot)
        pack_pair(jnp.where(valid, back, 0.0), G, pair)
        return carry

    lax.fori_loop(0, DP // 2, norm_body, 0)
    send(G)
    gate_store = pltpu.make_async_copy(gstage, gate_grad.at[0, 0], store_sem.at[0])
    gate_store.start()
    pack(V, 5)
    send(V)

    lane768 = lax.broadcasted_iota(jnp.int32, (1, DP * PACK), 1)
    lane512 = lax.broadcasted_iota(jnp.int32, (1, 2 * ROWS), 1)
    side48 = jnp.where(row48 < SLOT, 0, 1)
    slot48 = row48 - side48 * SLOT

    def target_body(d, carry):
        begin, where_to = carry
        count = plan[dp, 0, d]
        i = lane768 - d * PACK
        side = jnp.where(i < SLOT, 0, 1)
        j = i - side * SLOT
        hit = (i >= 0) & (i < PACK) & (j < count)
        where_to = jnp.where(hit, side * ROWS + begin + j, where_to)
        at = jnp.where(slot48 < count, side48 * ROWS + begin + slot48, -1)
        spread[pl.ds(pl.multiple_of(d * PACK, PACK), PACK), :] = (
            jnp.where(lane512 == at, 1.0, 0.0).astype(BF16)
        )
        return begin + count, where_to

    _, where_to = lax.fori_loop(
        0, DP, target_body, (jnp.int32(0), jnp.full((1, DP * PACK), -1, jnp.int32))
    )

    def place_body(i, carry):
        at = pl.multiple_of(i * 64, 64)
        rows = lax.broadcasted_iota(jnp.int32, (64, 1), 0) + at
        place[pl.ds(at, 64), :] = jnp.where(rows == where_to, 1.0, 0.0).astype(BF16)
        return carry

    lax.fori_loop(0, 2 * ROWS // 64, place_body, 0)

    pattern = block_mask[0].astype(F32)
    block_row = lax.broadcasted_iota(jnp.int32, (NBLK, LEN), 0)
    pos = lax.broadcasted_iota(jnp.int32, (NBLK, LEN), 1)
    onehot = jnp.where(block_row == pos // DH, 1.0, 0.0)
    kept = lax.dot_general(
        pattern, onehot, (((0,), (0,)), ((), ())), preferred_element_type=F32
    )
    length = hist_len[0]
    total = jnp.full((NBLK, LEN), length, jnp.int32).astype(F32)
    inverse = 1.0 / jnp.sqrt(total)
    live[...] = jnp.where(
        ((kept > 0.5) | (onehot > 0.5)) & (pos < length), inverse, 0.0
    )

    def gather_rows(array, half):
        chunk = 2 * array + half
        landed(drecv.at[chunk], drecv_sem.at[chunk])
        block = drecv[chunk].reshape(DP * PACK, QUART)
        comp[chunk] = jnp.dot(place[...], block, preferred_element_type=F32).astype(
            BF16
        )
        for to in range(4):
            src = comp.at[
                chunk, pl.ds(to // 2 * ROWS, ROWS), pl.ds(to % 2 * DH, DH)
            ]
            dst = hist.at[array, sq]
            peer = 2 * to + half

            @pl.when(sq != peer)
            def _():
                remote(
                    src, dst, ssend_sem.at[array], srecv_sem.at[array], (dp, peer)
                ).start()

            @pl.when(sq == peer)
            def _():
                pltpu.make_async_copy(src, dst, srecv_sem.at[array]).start()

    def history(array):
        landed(hist.at[array], srecv_sem.at[array])

    nt = (((1,), (1,)), ((), ()))

    def tile_rows(array, i):
        return hist[array, pl.ds(2 * i, 2)].reshape(TILE, DH)

    def scores_tile(i, j, diagonal):
        cols = pl.ds(pl.multiple_of(j * TILE, TILE), TILE)
        query = tile_rows(Q, j)
        key = tile_rows(K, i)
        for part in range(TILE // DH):
            base = part * DH
            raw = lax.dot_general(
                key[base : base + DH], query, nt, preferred_element_type=F32
            )
            scores = raw * SCALE
            sig = 0.5 * jnp.tanh(raw * (0.5 * SCALE)) + 0.5
            keep = live[pl.ds(TILE // DH * i + part, 1), cols]
            if diagonal:
                s = lax.broadcasted_iota(jnp.int32, (DH, TILE), 0) + base
                t = lax.broadcasted_iota(jnp.int32, (DH, TILE), 1)
                keep = jnp.where(s <= t, keep, 0.0)
            fac = sig * keep
            weight = scores * fac
            rows = pl.ds(pl.multiple_of(i * TILE + base, DH), DH)
            wt[rows, cols] = weight.astype(BF16)
            dt[rows, cols] = fac + weight * (1.0 - sig)

    def scores_strip(i, carry):
        scores_tile(i, i, True)

        def body(j, c):
            scores_tile(i, j, False)
            return c

        lax.fori_loop(i + 1, TILES, body, 0)
        return carry

    def later_sum(out, array, scale):
        for i in range(TILES):
            acc = jnp.dot(
                wt[i * TILE : (i + 1) * TILE, i * TILE :],
                hist[array, 2 * i :].reshape(LEN - i * TILE, DH),
                preferred_element_type=F32,
            )
            grads[out, 2 * i : 2 * i + 2] = (
                (acc * scale).astype(BF16).reshape(2, ROWS, DH)
            )

    def score_grad_strip(i, carry):
        rows = pl.ds(pl.multiple_of(i * TILE, TILE), TILE)
        value = tile_rows(V, i)

        def body(j, c):
            cols = pl.ds(pl.multiple_of(j * TILE, TILE), TILE)
            products = lax.dot_general(
                value, tile_rows(G, j), nt, preferred_element_type=F32
            )
            wt[rows, cols] = (products * dt[rows, cols]).astype(BF16)
            return c

        lax.fori_loop(i, TILES, body, 0)
        return carry

    def query_sum():
        for j in range(TILES):
            acc = jnp.dot(
                key_t[:, : (j + 1) * TILE],
                wt[: (j + 1) * TILE, j * TILE : (j + 1) * TILE],
                preferred_element_type=F32,
            )
            grads[DQ, 2 * j : 2 * j + 2] = (
                (acc * SCALE).T.astype(BF16).reshape(2, ROWS, DH)
            )

    def send_grads(out):
        def body(k, carry):
            peer = lax.rem(sq + 4 + k, SEQ)
            src = grads.at[out, peer]
            dst = gath.at[
                2 * out + core,
                zed // 2,
                :,
                pl.ds(pl.multiple_of(lax.rem(zed, 2) * DH, DH), DH),
            ]
            recv_sem = grecv_sem.at[2 * out + core]

            @pl.when(k != 4)
            def _():
                remote(src, dst, gsend_sem.at[out], recv_sem, (dp, peer)).start()

            @pl.when(k == 4)
            def _():
                pltpu.make_async_copy(src, dst, recv_sem).start()

            return carry

        lax.fori_loop(0, SEQ, body, 0)

    def return_rows(out):
        for half in range(2):
            chunk = 2 * out + half
            landed(gath.at[chunk], grecv_sem.at[chunk])
            block = gath[chunk].reshape(2 * ROWS, QUART)
            osend[chunk] = (
                jnp.dot(spread[...], block, preferred_element_type=F32)
                .astype(BF16)
                .reshape(DP, PACK, QUART)
            )
            scatter_dp(osend, orecv, osend_sem, orecv_sem, chunk)

    stores = []

    def finish(out, target):
        for half in range(2):
            chunk = 2 * out + half
            landed(orecv.at[chunk], orecv_sem.at[chunk])

            def body(pair, carry):
                at = pl.multiple_of(pair * PACK, PACK)
                one = orecv[chunk, 2 * pair].astype(F32)
                two = orecv[chunk, 2 * pair + 1].astype(F32)
                lo = jnp.concatenate([one[:SLOT], two[:SLOT]], axis=0)
                hi = jnp.concatenate([one[SLOT:], two[SLOT:]], axis=0)
                base = half * HALF
                ostage[out, pl.ds(at, PACK), base : base + QUART] = lo.astype(BF16)
                ostage[out, pl.ds(at, PACK), base + QUART : base + HALF] = hi.astype(BF16)
                return carry

            lax.fori_loop(0, DP // 2, body, 0)
            store = pltpu.make_async_copy(
                ostage.at[out, :, pl.ds(half * HALF, HALF)],
                target.at[0, 0, :, pl.ds(half * HALF, HALF)],
                store_sem.at[1 + chunk],
            )
            store.start()
            stores.append(store)

    gather_rows(Q, 0)
    gather_rows(Q, 1)
    gather_rows(K, 0)
    gather_rows(K, 1)
    gather_rows(G, 0)
    history(Q)
    history(K)
    lax.fori_loop(0, 1, scores_strip, 0)
    gather_rows(G, 1)
    lax.fori_loop(1, TILES, scores_strip, 0)
    history(G)
    later_sum(DV, G, 1.0)
    send_grads(DV)
    gather_rows(V, 0)
    gather_rows(V, 1)
    key_t[...] = hist[K].reshape(LEN, DH).astype(F32).T.astype(BF16)
    return_rows(DV)
    history(V)
    lax.fori_loop(0, TILES, score_grad_strip, 0)
    later_sum(DK, Q, SCALE)
    send_grads(DK)
    query_sum()
    send_grads(DQ)
    return_rows(DK)
    return_rows(DQ)
    finish(DV, value_grad)
    finish(DK, key_grad)
    finish(DQ, query_grad)

    for chunk in range(8):
        left(dsend.at[chunk, pl.ds(0, DP - 1)], dsend_sem.at[chunk])
    for array in range(4):
        left(hist.at[array, pl.ds(0, SEQ - 1)], ssend_sem.at[array])
    for out in range(3):
        left(grads.at[out, pl.ds(0, SEQ - 1)], gsend_sem.at[out])
    for chunk in range(6):
        left(osend.at[chunk, pl.ds(0, DP - 1)], osend_sem.at[chunk])
    gate_store.wait()
    for store in stores:
        store.wait()


def local(queries, keys, values, gates, attended, out_grad, plan, hist_len, block_mask):
    hbm = pl.BlockSpec(memory_space=pl.ANY)
    smem = pl.BlockSpec(memory_space=pltpu.SMEM)
    vmem = pl.BlockSpec(memory_space=pltpu.VMEM)
    out = jax.ShapeDtypeStruct((1, 1, CAP, WIDTH), BF16)
    dma = pltpu.SemaphoreType.DMA
    return pl.pallas_call(
        kernel,
        out_shape=(out,) * 4,
        in_specs=[hbm] * 6 + [smem, smem, vmem],
        out_specs=(hbm,) * 4,
        scratch_shapes=[
            pltpu.VMEM((6, CAP, WIDTH), BF16),
            pltpu.VMEM((8, DP, PACK, QUART), BF16),
            pltpu.VMEM((8, DP, PACK, QUART), BF16),
            pltpu.VMEM((8, 2 * ROWS, QUART), BF16),
            pltpu.VMEM((4, SEQ, ROWS, DH), BF16),
            pltpu.VMEM((NBLK, LEN), F32),
            pltpu.VMEM((LEN, LEN), BF16),
            pltpu.VMEM((LEN, LEN), F32),
            pltpu.VMEM((DH, LEN), BF16),
            pltpu.VMEM((3, SEQ, ROWS, DH), BF16),
            pltpu.VMEM((6, 2, ROWS, QUART), BF16),
            pltpu.VMEM((6, DP, PACK, QUART), BF16),
            pltpu.VMEM((6, DP, PACK, QUART), BF16),
            pltpu.VMEM((3, CAP, WIDTH), BF16),
            pltpu.VMEM((CAP, WIDTH), BF16),
            pltpu.VMEM((2 * ROWS, DP * PACK), BF16),
            pltpu.VMEM((DP * PACK, 2 * ROWS), BF16),
            dma((6,)),
            dma((7,)),
            dma((8,)),
            dma((8,)),
            dma((4,)),
            dma((4,)),
            dma((3,)),
            dma((6,)),
            dma((6,)),
            dma((6,)),
        ],
        compiler_params=pltpu.CompilerParams(
            collective_id=1, has_side_effects=True, vmem_limit_bytes=60 * 2**20
        ),
    )(queries, keys, values, gates, attended, out_grad, plan, hist_len, block_mask)


def solution(mesh):
    rows = P("dp", "seq", None, None)
    return jax.shard_map(
        local,
        mesh=mesh,
        in_specs=(rows,) * 6 + (P(None, "seq", None), P("dp"), P("dp", None, None)),
        out_specs=(rows,) * 4,
        check_vma=False,
    )
```

```python
import jax
import jax.numpy as jnp
from jax import lax
from jax.experimental import pallas as pl
from jax.experimental.pallas import tpu as pltpu
from jax.sharding import PartitionSpec as P

MESH = pl.DeviceIdType.MESH
F32 = jnp.float32
BF16 = jnp.bfloat16

DP = 16
SEQ = 8
SLOT = 24
CAP = 384
WIDTH = 1024
ROWS = 256
DH = 128
LEN = 2048
NBLK = 16
PACK = 2 * SLOT
HALF = 512
QUART = 256
SCALE = DH ** (-0.5)
TILE = 512
TILES = LEN // TILE

Q, K, G, V = 0, 1, 2, 3
DV, DK, DQ = 0, 1, 2


def kernel(
    queries,
    keys,
    values,
    gates,
    attended,
    out_grad,
    plan,
    hist_len,
    block_mask,
    orecv,
    gate_grad,
    stage,
    dsend,
    drecv,
    comp,
    hist,
    live,
    wt,
    dt,
    key_t,
    grads,
    gath,
    osend,
    gstage,
    place,
    spread,
    load_sem,
    store_sem,
    dsend_sem,
    drecv_sem,
    ssend_sem,
    srecv_sem,
    gsend_sem,
    grecv_sem,
    osend_sem,
    orecv_sem,
):
    dp = lax.axis_index("dp")
    sq = lax.axis_index("seq")
    row_x, row_y = dp // 4, lax.rem(dp, 4)
    zed, core = sq // 2, lax.rem(sq, 2)

    barrier = pltpu.get_barrier_semaphore()

    def greet_dp(k, carry):
        pl.semaphore_signal(
            barrier, inc=1, device_id=(lax.rem(dp + k, DP), sq), device_id_type=MESH
        )
        return carry

    def greet_seq(k, carry):
        pl.semaphore_signal(
            barrier, inc=1, device_id=(dp, lax.rem(sq + k, SEQ)), device_id_type=MESH
        )
        return carry

    sources = (queries, keys, attended, gates, out_grad, values)
    loads = [
        pltpu.make_async_copy(src.at[0, 0], stage.at[i], load_sem.at[i])
        for i, src in enumerate(sources)
    ]
    for load in loads:
        load.start()

    lax.fori_loop(1, DP, greet_dp, 0)
    lax.fori_loop(1, SEQ, greet_seq, 0)

    def remote(src, dst, send_sem, recv_sem, target):
        return pltpu.make_async_remote_copy(
            src_ref=src,
            dst_ref=dst,
            send_sem=send_sem,
            recv_sem=recv_sem,
            device_id=target,
            device_id_type=MESH,
        )

    def landed(ref, sem):
        remote(ref, ref, sem, sem, (dp, sq)).wait_recv()

    def left(ref, sem):
        remote(ref, ref, sem, sem, (dp, sq)).wait_send()

    def scatter_dp(src, dst, send_sems, recv_sems, chunk):
        def body(k, carry):
            off = k ^ 10
            peer = lax.rem(row_x + off // 4, 4) * 4 + lax.rem(row_y + lax.rem(off, 4), 4)

            @pl.when(k != 10)
            def _():
                remote(
                    src.at[chunk, peer],
                    dst.at[chunk, dp],
                    send_sems.at[chunk],
                    recv_sems.at[chunk],
                    (peer, sq),
                ).start()

            @pl.when(k == 10)
            def _():
                pltpu.make_async_copy(
                    src.at[chunk, dp], dst.at[chunk, dp], recv_sems.at[chunk]
                ).start()

            return carry

        lax.fori_loop(0, DP, body, 0)

    def pack_pair(block, array, pair):
        for half in range(2):
            for side in range(2):
                part = block[side * SLOT : (side + 1) * SLOT]
                at = half * HALF
                message = jnp.concatenate(
                    [part[:, at : at + QUART], part[:, at + QUART : at + HALF]], axis=0
                )
                dsend[2 * array + half, 2 * pair + side] = message.astype(BF16)

    def pack(array, slot):
        loads[slot].wait()

        def body(pair, carry):
            at = pl.multiple_of(pair * PACK, PACK)
            pack_pair(stage[slot, pl.ds(at, PACK), :].astype(F32), array, pair)
            return carry

        lax.fori_loop(0, DP // 2, body, 0)

    def send(array, half):
        scatter_dp(dsend, drecv, dsend_sem, drecv_sem, 2 * array + half)

    pack(Q, 0)
    pl.semaphore_wait(barrier, DP - 1 + SEQ - 1)
    send(Q, 0)
    pack(K, 1)
    send(K, 0)

    for i in (2, 3, 4):
        loads[i].wait()
    row48 = lax.broadcasted_iota(jnp.int32, (PACK, 1), 0)

    def norm_body(pair, carry):
        at = pl.multiple_of(pair * PACK, PACK)
        inputs = stage[2, pl.ds(at, PACK), :].astype(F32)
        gate = stage[3, pl.ds(at, PACK), :].astype(F32)
        grad = stage[4, pl.ds(at, PACK), :].astype(F32)
        center = inputs - jnp.mean(inputs, axis=-1, keepdims=True)
        spread_ = jnp.mean(center * center, axis=-1, keepdims=True)
        inv = lax.rsqrt(spread_ + 1e-05)
        normed = center * inv
        first = plan[2 * pair, 0, dp]
        second = plan[2 * pair + 1, 0, dp]
        valid = row48 < jnp.where(row48 < SLOT, first, SLOT + second)
        gstage[pl.ds(at, PACK), :] = jnp.where(valid, grad * normed, 0.0).astype(BF16)
        cot = grad * gate
        mean_cot = jnp.mean(cot, axis=-1, keepdims=True)
        mean_dot = jnp.mean(cot * normed, axis=-1, keepdims=True)
        back = inv * (cot - mean_cot - normed * mean_dot)
        pack_pair(jnp.where(valid, back, 0.0), G, pair)
        return carry

    lax.fori_loop(0, DP // 2, norm_body, 0)
    send(G, 0)
    gate_store = pltpu.make_async_copy(gstage, gate_grad, store_sem.at[0])
    gate_store.start()
    pack(V, 5)
    send(V, 0)

    lane768 = lax.broadcasted_iota(jnp.int32, (1, DP * PACK), 1)
    lane512 = lax.broadcasted_iota(jnp.int32, (1, 2 * ROWS), 1)
    side48 = jnp.where(row48 < SLOT, 0, 1)
    slot48 = row48 - side48 * SLOT

    def target_body(d, carry):
        begin, where_to = carry
        count = plan[dp, 0, d]
        i = lane768 - d * PACK
        side = jnp.where(i < SLOT, 0, 1)
        j = i - side * SLOT
        hit = (i >= 0) & (i < PACK) & (j < count)
        where_to = jnp.where(hit, side * ROWS + begin + j, where_to)
        at = jnp.where(slot48 < count, side48 * ROWS + begin + slot48, -1)
        spread[pl.ds(pl.multiple_of(d * PACK, PACK), PACK), :] = (
            jnp.where(lane512 == at, 1.0, 0.0).astype(BF16)
        )
        return begin + count, where_to

    _, where_to = lax.fori_loop(
        0, DP, target_body, (jnp.int32(0), jnp.full((1, DP * PACK), -1, jnp.int32))
    )

    def place_body(i, carry):
        at = pl.multiple_of(i * 64, 64)
        rows = lax.broadcasted_iota(jnp.int32, (64, 1), 0) + at
        place[pl.ds(at, 64), :] = jnp.where(rows == where_to, 1.0, 0.0).astype(BF16)
        return carry

    lax.fori_loop(0, 2 * ROWS // 64, place_body, 0)

    pattern = block_mask[0].astype(F32)
    block_row = lax.broadcasted_iota(jnp.int32, (NBLK, LEN), 0)
    pos = lax.broadcasted_iota(jnp.int32, (NBLK, LEN), 1)
    onehot = jnp.where(block_row == pos // DH, 1.0, 0.0)
    kept = lax.dot_general(
        pattern, onehot, (((0,), (0,)), ((), ())), preferred_element_type=F32
    )
    length = hist_len[0]
    total = jnp.full((NBLK, LEN), length, jnp.int32).astype(F32)
    inverse = 1.0 / jnp.sqrt(total)
    live[...] = jnp.where(
        ((kept > 0.5) | (onehot > 0.5)) & (pos < length), inverse, 0.0
    )

    def gather_rows(array, half):
        chunk = 2 * array + half
        landed(drecv.at[chunk], drecv_sem.at[chunk])
        block = drecv[chunk].reshape(DP * PACK, QUART)
        comp[chunk] = jnp.dot(place[...], block, preferred_element_type=F32).astype(
            BF16
        )
        for to in range(4):
            src = comp.at[
                chunk, pl.ds(to // 2 * ROWS, ROWS), pl.ds(to % 2 * DH, DH)
            ]
            dst = hist.at[array, sq]
            peer = 2 * to + half

            @pl.when(sq != peer)
            def _():
                remote(
                    src, dst, ssend_sem.at[array], srecv_sem.at[array], (dp, peer)
                ).start()

            @pl.when(sq == peer)
            def _():
                pltpu.make_async_copy(src, dst, srecv_sem.at[array]).start()

    def history(array):
        landed(hist.at[array], srecv_sem.at[array])

    nt = (((1,), (1,)), ((), ()))

    def tile_rows(array, i):
        return hist[array, pl.ds(2 * i, 2)].reshape(TILE, DH)

    def scores_tile(i, j, diagonal):
        cols = pl.ds(pl.multiple_of(j * TILE, TILE), TILE)
        query = tile_rows(Q, j)
        key = tile_rows(K, i)
        for part in range(TILE // DH):
            base = part * DH
            raw = lax.dot_general(
                key[base : base + DH], query, nt, preferred_element_type=F32
            )
            scores = raw * SCALE
            sig = 0.5 * jnp.tanh(raw * (0.5 * SCALE)) + 0.5
            keep = live[pl.ds(TILE // DH * i + part, 1), cols]
            if diagonal:
                s = lax.broadcasted_iota(jnp.int32, (DH, TILE), 0) + base
                t = lax.broadcasted_iota(jnp.int32, (DH, TILE), 1)
                keep = jnp.where(s <= t, keep, 0.0)
            fac = sig * keep
            weight = scores * fac
            rows = pl.ds(pl.multiple_of(i * TILE + base, DH), DH)
            wt[rows, cols] = weight.astype(BF16)
            dt[rows, cols] = fac + weight * (1.0 - sig)

    def scores_strip(i, carry):
        scores_tile(i, i, True)

        def body(j, c):
            scores_tile(i, j, False)
            return c

        lax.fori_loop(i + 1, TILES, body, 0)
        return carry

    def later_sum(out, array, scale):
        for i in range(TILES):
            acc = jnp.dot(
                wt[i * TILE : (i + 1) * TILE, i * TILE :],
                hist[array, 2 * i :].reshape(LEN - i * TILE, DH),
                preferred_element_type=F32,
            )
            grads[out, 2 * i : 2 * i + 2] = (
                (acc * scale).astype(BF16).reshape(2, ROWS, DH)
            )

    def score_grad_strip(i, carry):
        rows = pl.ds(pl.multiple_of(i * TILE, TILE), TILE)
        value = tile_rows(V, i)

        def body(j, c):
            cols = pl.ds(pl.multiple_of(j * TILE, TILE), TILE)
            products = lax.dot_general(
                value, tile_rows(G, j), nt, preferred_element_type=F32
            )
            wt[rows, cols] = (products * dt[rows, cols]).astype(BF16)
            return c

        lax.fori_loop(i, TILES, body, 0)
        return carry

    def query_sum():
        key_t[...] = hist[K].reshape(LEN, DH).astype(F32).T.astype(BF16)
        for j in range(TILES):
            acc = jnp.dot(
                key_t[:, : (j + 1) * TILE],
                wt[: (j + 1) * TILE, j * TILE : (j + 1) * TILE],
                preferred_element_type=F32,
            )
            grads[DQ, 2 * j : 2 * j + 2] = (
                (acc * SCALE).T.astype(BF16).reshape(2, ROWS, DH)
            )

    def send_grads(out):
        def body(k, carry):
            peer = lax.rem(sq + 4 + k, SEQ)
            src = grads.at[out, peer]
            dst = gath.at[
                2 * out + core,
                zed // 2,
                :,
                pl.ds(pl.multiple_of(lax.rem(zed, 2) * DH, DH), DH),
            ]
            recv_sem = grecv_sem.at[2 * out + core]

            @pl.when(k != 4)
            def _():
                remote(src, dst, gsend_sem.at[out], recv_sem, (dp, peer)).start()

            @pl.when(k == 4)
            def _():
                pltpu.make_async_copy(src, dst, recv_sem).start()

            return carry

        lax.fori_loop(0, SEQ, body, 0)

    def return_rows(out, half):
        chunk = 2 * out + half
        landed(gath.at[chunk], grecv_sem.at[chunk])
        block = gath[chunk].reshape(2 * ROWS, QUART)
        osend[chunk] = (
            jnp.dot(spread[...], block, preferred_element_type=F32)
            .astype(BF16)
            .reshape(DP, PACK, QUART)
        )
        scatter_dp(osend, orecv, osend_sem, orecv_sem, chunk)

    gather_rows(Q, 0)
    send(Q, 1)
    gather_rows(K, 0)
    send(K, 1)
    gather_rows(G, 0)
    send(G, 1)

    @pl.when(core == 0)
    def _():
        history(Q)
        history(K)
        lax.fori_loop(0, 1, scores_strip, 0)

    gather_rows(V, 0)
    send(V, 1)

    @pl.when(core == 0)
    def _():
        lax.fori_loop(1, TILES, scores_strip, 0)
        history(G)
        later_sum(DV, G, 1.0)
        send_grads(DV)

    gather_rows(Q, 1)

    @pl.when(core == 0)
    def _():
        history(V)
        lax.fori_loop(0, TILES, score_grad_strip, 0)
        later_sum(DK, Q, SCALE)
        send_grads(DK)

    gather_rows(K, 1)

    @pl.when(core == 0)
    def _():
        query_sum()
        send_grads(DQ)

    gather_rows(G, 1)

    @pl.when(core == 1)
    def _():
        history(Q)
        history(K)
        lax.fori_loop(0, 1, scores_strip, 0)

    gather_rows(V, 1)
    return_rows(DV, 0)
    return_rows(DK, 0)

    @pl.when(core == 1)
    def _():
        lax.fori_loop(1, TILES, scores_strip, 0)
        history(G)
        later_sum(DV, G, 1.0)
        send_grads(DV)

    return_rows(DQ, 0)

    @pl.when(core == 1)
    def _():
        history(V)
        lax.fori_loop(0, TILES, score_grad_strip, 0)
        later_sum(DK, Q, SCALE)
        send_grads(DK)
        query_sum()
        send_grads(DQ)

    return_rows(DV, 1)
    return_rows(DK, 1)
    return_rows(DQ, 1)

    for chunk in range(8):
        left(dsend.at[chunk, pl.ds(0, DP - 1)], dsend_sem.at[chunk])
    for array in range(4):
        left(hist.at[array, pl.ds(0, SEQ - 1)], ssend_sem.at[array])
    for out in range(3):
        left(grads.at[out, pl.ds(0, SEQ - 1)], gsend_sem.at[out])
    for chunk in range(6):
        landed(orecv.at[chunk], orecv_sem.at[chunk])
        left(osend.at[chunk, pl.ds(0, DP - 1)], osend_sem.at[chunk])
    gate_store.wait()


def unpack(
    moved, gate_in, query_grad, key_grad, value_grad, gate_grad, block, ready, gate, load_sem, store_sem
):
    loads = [
        pltpu.make_async_copy(moved.at[chunk], block.at[chunk], load_sem.at[chunk])
        for chunk in range(6)
    ]
    loads.append(pltpu.make_async_copy(gate_in, gate, load_sem.at[6]))
    for load in loads:
        load.start()
    stores = []
    for chunk in range(6):
        loads[chunk].wait()

        def body(pair, carry):
            at = pl.multiple_of(pair * PACK, PACK)
            one = block[chunk, 2 * pair].astype(F32)
            two = block[chunk, 2 * pair + 1].astype(F32)
            lo = jnp.concatenate([one[:SLOT], two[:SLOT]], axis=0)
            hi = jnp.concatenate([one[SLOT:], two[SLOT:]], axis=0)
            ready[chunk, pl.ds(at, PACK), :QUART] = lo.astype(BF16)
            ready[chunk, pl.ds(at, PACK), QUART:] = hi.astype(BF16)
            return carry

        lax.fori_loop(0, DP // 2, body, 0, unroll=True)
        target = (value_grad, key_grad, query_grad)[chunk // 2]
        store = pltpu.make_async_copy(
            ready.at[chunk],
            target.at[0, 0, :, pl.ds(chunk % 2 * HALF, HALF)],
            store_sem.at[chunk],
        )
        store.start()
        stores.append(store)
    loads[6].wait()
    store = pltpu.make_async_copy(gate, gate_grad.at[0, 0], store_sem.at[6])
    store.start()
    stores.append(store)
    for store in stores:
        store.wait()


def local(queries, keys, values, gates, attended, out_grad, plan, hist_len, block_mask):
    hbm = pl.BlockSpec(memory_space=pl.ANY)
    smem = pl.BlockSpec(memory_space=pltpu.SMEM)
    vmem = pl.BlockSpec(memory_space=pltpu.VMEM)
    out = jax.ShapeDtypeStruct((1, 1, CAP, WIDTH), BF16)
    arrived = jax.ShapeDtypeStruct((6, DP, PACK, QUART), BF16)
    gate_out = jax.ShapeDtypeStruct((CAP, WIDTH), BF16)
    dma = pltpu.SemaphoreType.DMA
    moved, gate_grad = pl.pallas_call(
        kernel,
        out_shape=(arrived, gate_out),
        in_specs=[hbm] * 6 + [smem, smem, vmem],
        out_specs=(hbm,) * 2,
        scratch_shapes=[
            pltpu.VMEM((6, CAP, WIDTH), BF16),
            pltpu.VMEM((8, DP, PACK, QUART), BF16),
            pltpu.VMEM((8, DP, PACK, QUART), BF16),
            pltpu.VMEM((8, 2 * ROWS, QUART), BF16),
            pltpu.VMEM((4, SEQ, ROWS, DH), BF16),
            pltpu.VMEM((NBLK, LEN), F32),
            pltpu.VMEM((LEN, LEN), BF16),
            pltpu.VMEM((LEN, LEN), F32),
            pltpu.VMEM((DH, LEN), BF16),
            pltpu.VMEM((3, SEQ, ROWS, DH), BF16),
            pltpu.VMEM((6, 2, ROWS, QUART), BF16),
            pltpu.VMEM((6, DP, PACK, QUART), BF16),
            pltpu.VMEM((CAP, WIDTH), BF16),
            pltpu.VMEM((2 * ROWS, DP * PACK), BF16),
            pltpu.VMEM((DP * PACK, 2 * ROWS), BF16),
            dma((6,)),
            dma((1,)),
            dma((8,)),
            dma((8,)),
            dma((4,)),
            dma((4,)),
            dma((3,)),
            dma((6,)),
            dma((6,)),
            dma((6,)),
        ],
        compiler_params=pltpu.CompilerParams(
            collective_id=1, has_side_effects=True, vmem_limit_bytes=60 * 2**20
        ),
    )(queries, keys, values, gates, attended, out_grad, plan, hist_len, block_mask)
    return pl.pallas_call(
        unpack,
        out_shape=(out,) * 4,
        in_specs=[hbm] * 2,
        out_specs=(hbm,) * 4,
        scratch_shapes=[
            pltpu.VMEM((6, DP, PACK, QUART), BF16),
            pltpu.VMEM((6, CAP, HALF), BF16),
            pltpu.VMEM((CAP, WIDTH), BF16),
            dma((7,)),
            dma((7,)),
        ],
        compiler_params=pltpu.CompilerParams(vmem_limit_bytes=60 * 2**20),
    )(moved, gate_grad)


def solution(mesh):
    rows = P("dp", "seq", None, None)
    return jax.shard_map(
        local,
        mesh=mesh,
        in_specs=(rows,) * 6 + (P(None, "seq", None), P("dp"), P("dp", None, None)),
        out_specs=(rows,) * 4,
        check_vma=False,
    )
```

```python
import jax
import jax.numpy as jnp
from jax import lax
from jax.experimental import pallas as pl
from jax.experimental.pallas import tpu as pltpu
from jax.sharding import PartitionSpec as P

MESH = pl.DeviceIdType.MESH
F32 = jnp.float32
BF16 = jnp.bfloat16

DP = 16
SEQ = 8
SLOT = 24
CAP = 384
WIDTH = 1024
ROWS = 256
DH = 128
LEN = 2048
NBLK = 16
PACK = 2 * SLOT
HALF = 512
QUART = 256
SCALE = DH ** (-0.5)
TILE = 512
TILES = LEN // TILE

Q, K, G, V = 0, 1, 2, 3
DV, DK, DQ = 0, 1, 2


def kernel(
    queries,
    keys,
    values,
    gates,
    attended,
    out_grad,
    plan,
    hist_len,
    block_mask,
    orecv,
    gate_grad,
    stage,
    dsend,
    drecv,
    comp,
    hist,
    live,
    wt,
    dt,
    key_t,
    grads,
    gath,
    osend,
    gstage,
    place,
    spread,
    load_sem,
    store_sem,
    dsend_sem,
    drecv_sem,
    ssend_sem,
    srecv_sem,
    gsend_sem,
    grecv_sem,
    osend_sem,
    orecv_sem,
):
    dp = lax.axis_index("dp")
    sq = lax.axis_index("seq")
    row_x, row_y = dp // 4, lax.rem(dp, 4)
    zed, core = sq // 2, lax.rem(sq, 2)

    barrier = pltpu.get_barrier_semaphore()

    def greet_dp(k, carry):
        pl.semaphore_signal(
            barrier, inc=1, device_id=(lax.rem(dp + k, DP), sq), device_id_type=MESH
        )
        return carry

    def greet_seq(k, carry):
        pl.semaphore_signal(
            barrier, inc=1, device_id=(dp, lax.rem(sq + k, SEQ)), device_id_type=MESH
        )
        return carry

    sources = (queries, keys, attended, gates, out_grad, values)
    loads = [
        pltpu.make_async_copy(src.at[0, 0], stage.at[i], load_sem.at[i])
        for i, src in enumerate(sources)
    ]
    for load in loads:
        load.start()

    lax.fori_loop(1, DP, greet_dp, 0)
    lax.fori_loop(1, SEQ, greet_seq, 0)

    def remote(src, dst, send_sem, recv_sem, target):
        return pltpu.make_async_remote_copy(
            src_ref=src,
            dst_ref=dst,
            send_sem=send_sem,
            recv_sem=recv_sem,
            device_id=target,
            device_id_type=MESH,
        )

    def landed(ref, sem):
        remote(ref, ref, sem, sem, (dp, sq)).wait_recv()

    def left(ref, sem):
        remote(ref, ref, sem, sem, (dp, sq)).wait_send()

    def scatter_dp(src, dst, send_sems, recv_sems, chunk):
        def body(k, carry):
            off = k ^ 10
            peer = lax.rem(row_x + off // 4, 4) * 4 + lax.rem(row_y + lax.rem(off, 4), 4)

            @pl.when(k != 10)
            def _():
                remote(
                    src.at[chunk, peer],
                    dst.at[chunk, dp],
                    send_sems.at[chunk],
                    recv_sems.at[chunk],
                    (peer, sq),
                ).start()

            @pl.when(k == 10)
            def _():
                pltpu.make_async_copy(
                    src.at[chunk, dp], dst.at[chunk, dp], recv_sems.at[chunk]
                ).start()

            return carry

        lax.fori_loop(0, DP, body, 0)

    def pack_pair(block, array, pair):
        for half in range(2):
            for side in range(2):
                part = block[side * SLOT : (side + 1) * SLOT]
                at = half * HALF
                message = jnp.concatenate(
                    [part[:, at : at + QUART], part[:, at + QUART : at + HALF]], axis=0
                )
                dsend[2 * array + half, 2 * pair + side] = message.astype(BF16)

    def pack(array, slot):
        loads[slot].wait()

        def body(pair, carry):
            at = pl.multiple_of(pair * PACK, PACK)
            pack_pair(stage[slot, pl.ds(at, PACK), :].astype(F32), array, pair)
            return carry

        lax.fori_loop(0, DP // 2, body, 0)

    def send(array, half):
        scatter_dp(dsend, drecv, dsend_sem, drecv_sem, 2 * array + half)

    pack(Q, 0)
    pl.semaphore_wait(barrier, DP - 1 + SEQ - 1)
    send(Q, 0)
    pack(K, 1)
    send(K, 0)

    for i in (2, 3, 4):
        loads[i].wait()
    row48 = lax.broadcasted_iota(jnp.int32, (PACK, 1), 0)

    def norm_body(pair, carry):
        at = pl.multiple_of(pair * PACK, PACK)
        inputs = stage[2, pl.ds(at, PACK), :].astype(F32)
        gate = stage[3, pl.ds(at, PACK), :].astype(F32)
        grad = stage[4, pl.ds(at, PACK), :].astype(F32)
        center = inputs - jnp.mean(inputs, axis=-1, keepdims=True)
        spread_ = jnp.mean(center * center, axis=-1, keepdims=True)
        inv = lax.rsqrt(spread_ + 1e-05)
        normed = center * inv
        first = plan[2 * pair, 0, dp]
        second = plan[2 * pair + 1, 0, dp]
        valid = row48 < jnp.where(row48 < SLOT, first, SLOT + second)
        gstage[pl.ds(at, PACK), :] = jnp.where(valid, grad * normed, 0.0).astype(BF16)
        cot = grad * gate
        mean_cot = jnp.mean(cot, axis=-1, keepdims=True)
        mean_dot = jnp.mean(cot * normed, axis=-1, keepdims=True)
        back = inv * (cot - mean_cot - normed * mean_dot)
        pack_pair(jnp.where(valid, back, 0.0), G, pair)
        return carry

    lax.fori_loop(0, DP // 2, norm_body, 0)
    gate_store = pltpu.make_async_copy(gstage, gate_grad, store_sem.at[0])
    gate_store.start()
    pack(V, 5)

    lane768 = lax.broadcasted_iota(jnp.int32, (1, DP * PACK), 1)
    lane512 = lax.broadcasted_iota(jnp.int32, (1, 2 * ROWS), 1)
    side48 = jnp.where(row48 < SLOT, 0, 1)
    slot48 = row48 - side48 * SLOT

    def target_body(d, carry):
        begin, where_to = carry
        count = plan[dp, 0, d]
        i = lane768 - d * PACK
        side = jnp.where(i < SLOT, 0, 1)
        j = i - side * SLOT
        hit = (i >= 0) & (i < PACK) & (j < count)
        where_to = jnp.where(hit, side * ROWS + begin + j, where_to)
        at = jnp.where(slot48 < count, side48 * ROWS + begin + slot48, -1)
        spread[pl.ds(pl.multiple_of(d * PACK, PACK), PACK), :] = (
            jnp.where(lane512 == at, 1.0, 0.0).astype(BF16)
        )
        return begin + count, where_to

    _, where_to = lax.fori_loop(
        0, DP, target_body, (jnp.int32(0), jnp.full((1, DP * PACK), -1, jnp.int32))
    )

    def place_body(i, carry):
        at = pl.multiple_of(i * 64, 64)
        rows = lax.broadcasted_iota(jnp.int32, (64, 1), 0) + at
        place[pl.ds(at, 64), :] = jnp.where(rows == where_to, 1.0, 0.0).astype(BF16)
        return carry

    lax.fori_loop(0, 2 * ROWS // 64, place_body, 0)

    pattern = block_mask[0].astype(F32)
    block_row = lax.broadcasted_iota(jnp.int32, (NBLK, LEN), 0)
    pos = lax.broadcasted_iota(jnp.int32, (NBLK, LEN), 1)
    onehot = jnp.where(block_row == pos // DH, 1.0, 0.0)
    kept = lax.dot_general(
        pattern, onehot, (((0,), (0,)), ((), ())), preferred_element_type=F32
    )
    length = hist_len[0]
    total = jnp.full((NBLK, LEN), length, jnp.int32).astype(F32)
    inverse = 1.0 / jnp.sqrt(total)
    live[...] = jnp.where(
        ((kept > 0.5) | (onehot > 0.5)) & (pos < length), inverse, 0.0
    )

    def gather_rows(array, half):
        chunk = 2 * array + half
        landed(drecv.at[chunk], drecv_sem.at[chunk])
        block = drecv[chunk].reshape(DP * PACK, QUART)
        comp[chunk] = jnp.dot(place[...], block, preferred_element_type=F32).astype(
            BF16
        )
        for k in range(4):
            to = lax.rem(zed + 2 + k, 4)
            src = comp.at[
                chunk,
                pl.ds(pl.multiple_of(to // 2 * ROWS, ROWS), ROWS),
                pl.ds(pl.multiple_of(lax.rem(to, 2) * DH, DH), DH),
            ]
            dst = hist.at[array, sq]
            peer = 2 * to + half

            @pl.when(sq != peer)
            def _():
                remote(
                    src, dst, ssend_sem.at[array], srecv_sem.at[array], (dp, peer)
                ).start()

            @pl.when(sq == peer)
            def _():
                pltpu.make_async_copy(src, dst, srecv_sem.at[array]).start()

    def history(array):
        landed(hist.at[array], srecv_sem.at[array])

    nt = (((1,), (1,)), ((), ()))

    def tile_rows(array, i):
        return hist[array, pl.ds(2 * i, 2)].reshape(TILE, DH)

    def scores_tile(i, j, diagonal):
        cols = pl.ds(pl.multiple_of(j * TILE, TILE), TILE)
        query = tile_rows(Q, j)
        key = tile_rows(K, i)
        for part in range(TILE // DH):
            base = part * DH
            raw = lax.dot_general(
                key[base : base + DH], query, nt, preferred_element_type=F32
            )
            scores = raw * SCALE
            sig = 0.5 * jnp.tanh(raw * (0.5 * SCALE)) + 0.5
            keep = live[pl.ds(TILE // DH * i + part, 1), cols]
            if diagonal:
                s = lax.broadcasted_iota(jnp.int32, (DH, TILE), 0) + base
                t = lax.broadcasted_iota(jnp.int32, (DH, TILE), 1)
                keep = jnp.where(s <= t, keep, 0.0)
            fac = sig * keep
            weight = scores * fac
            rows = pl.ds(pl.multiple_of(i * TILE + base, DH), DH)
            wt[rows, cols] = weight.astype(BF16)
            dt[rows, cols] = fac + weight * (1.0 - sig)

    def scores_strip(i, carry):
        scores_tile(i, i, True)

        def body(j, c):
            scores_tile(i, j, False)
            return c

        lax.fori_loop(i + 1, TILES, body, 0)
        return carry

    def later_sum(out, array, scale):
        for i in range(TILES):
            acc = jnp.dot(
                wt[i * TILE : (i + 1) * TILE, i * TILE :],
                hist[array, 2 * i :].reshape(LEN - i * TILE, DH),
                preferred_element_type=F32,
            )
            grads[out, 2 * i : 2 * i + 2] = (
                (acc * scale).astype(BF16).reshape(2, ROWS, DH)
            )

    def score_grad_strip(i, carry):
        rows = pl.ds(pl.multiple_of(i * TILE, TILE), TILE)
        value = tile_rows(V, i)

        def body(j, c):
            cols = pl.ds(pl.multiple_of(j * TILE, TILE), TILE)
            products = lax.dot_general(
                value, tile_rows(G, j), nt, preferred_element_type=F32
            )
            wt[rows, cols] = (products * dt[rows, cols]).astype(BF16)
            return c

        lax.fori_loop(i, TILES, body, 0)
        return carry

    def query_sum():
        key_t[...] = hist[K].reshape(LEN, DH).astype(F32).T.astype(BF16)
        for j in range(TILES):
            acc = jnp.dot(
                key_t[:, : (j + 1) * TILE],
                wt[: (j + 1) * TILE, j * TILE : (j + 1) * TILE],
                preferred_element_type=F32,
            )
            grads[DQ, 2 * j : 2 * j + 2] = (
                (acc * SCALE).T.astype(BF16).reshape(2, ROWS, DH)
            )

    def send_grads(out):
        def body(k, carry):
            peer = lax.rem(sq + 4 + k, SEQ)
            src = grads.at[out, peer]
            dst = gath.at[
                2 * out + core,
                zed // 2,
                :,
                pl.ds(pl.multiple_of(lax.rem(zed, 2) * DH, DH), DH),
            ]
            recv_sem = grecv_sem.at[2 * out + core]

            @pl.when(k != 4)
            def _():
                remote(src, dst, gsend_sem.at[out], recv_sem, (dp, peer)).start()

            @pl.when(k == 4)
            def _():
                pltpu.make_async_copy(src, dst, recv_sem).start()

            return carry

        lax.fori_loop(0, SEQ, body, 0)

    def return_rows(out, half):
        chunk = 2 * out + half
        landed(gath.at[chunk], grecv_sem.at[chunk])
        block = gath[chunk].reshape(2 * ROWS, QUART)
        osend[chunk] = (
            jnp.dot(spread[...], block, preferred_element_type=F32)
            .astype(BF16)
            .reshape(DP, PACK, QUART)
        )
        scatter_dp(osend, orecv, osend_sem, orecv_sem, chunk)

    gather_rows(Q, 0)
    send(G, 0)
    gather_rows(K, 0)
    send(V, 0)
    gather_rows(G, 0)
    send(Q, 1)

    @pl.when(core == 0)
    def _():
        history(Q)
        history(K)
        lax.fori_loop(0, 1, scores_strip, 0)

    gather_rows(V, 0)
    send(K, 1)

    @pl.when(core == 0)
    def _():
        lax.fori_loop(1, TILES, scores_strip, 0)
        history(G)
        later_sum(DV, G, 1.0)
        send_grads(DV)

    gather_rows(Q, 1)
    send(G, 1)

    @pl.when(core == 0)
    def _():
        history(V)
        lax.fori_loop(0, TILES, score_grad_strip, 0)

    gather_rows(K, 1)
    send(V, 1)

    @pl.when(core == 0)
    def _():
        later_sum(DK, Q, SCALE)
        send_grads(DK)
        query_sum()
        send_grads(DQ)

    gather_rows(G, 1)

    @pl.when(core == 1)
    def _():
        history(Q)
        history(K)
        lax.fori_loop(0, 1, scores_strip, 0)

    gather_rows(V, 1)
    return_rows(DV, 0)
    return_rows(DK, 0)

    @pl.when(core == 1)
    def _():
        lax.fori_loop(1, TILES, scores_strip, 0)
        history(G)
        later_sum(DV, G, 1.0)
        send_grads(DV)

    return_rows(DQ, 0)

    @pl.when(core == 1)
    def _():
        history(V)
        lax.fori_loop(0, TILES, score_grad_strip, 0)
        later_sum(DK, Q, SCALE)
        send_grads(DK)
        query_sum()
        send_grads(DQ)

    return_rows(DV, 1)
    return_rows(DK, 1)
    return_rows(DQ, 1)

    for chunk in range(8):
        left(dsend.at[chunk, pl.ds(0, DP - 1)], dsend_sem.at[chunk])
    for array in range(4):
        left(hist.at[array, pl.ds(0, SEQ - 1)], ssend_sem.at[array])
    for out in range(3):
        left(grads.at[out, pl.ds(0, SEQ - 1)], gsend_sem.at[out])
    for chunk in range(6):
        landed(orecv.at[chunk], orecv_sem.at[chunk])
        left(osend.at[chunk, pl.ds(0, DP - 1)], osend_sem.at[chunk])
    gate_store.wait()


def unpack(
    moved, gate_in, query_grad, key_grad, value_grad, gate_grad, block, ready, gate, load_sem, store_sem
):
    loads = [
        pltpu.make_async_copy(moved.at[chunk], block.at[chunk], load_sem.at[chunk])
        for chunk in range(6)
    ]
    loads.append(pltpu.make_async_copy(gate_in, gate, load_sem.at[6]))
    for load in loads:
        load.start()
    stores = []
    for chunk in range(6):
        loads[chunk].wait()

        def body(pair, carry):
            at = pl.multiple_of(pair * PACK, PACK)
            one = block[chunk, 2 * pair].astype(F32)
            two = block[chunk, 2 * pair + 1].astype(F32)
            lo = jnp.concatenate([one[:SLOT], two[:SLOT]], axis=0)
            hi = jnp.concatenate([one[SLOT:], two[SLOT:]], axis=0)
            ready[chunk, pl.ds(at, PACK), :QUART] = lo.astype(BF16)
            ready[chunk, pl.ds(at, PACK), QUART:] = hi.astype(BF16)
            return carry

        lax.fori_loop(0, DP // 2, body, 0, unroll=True)
        target = (value_grad, key_grad, query_grad)[chunk // 2]
        store = pltpu.make_async_copy(
            ready.at[chunk],
            target.at[0, 0, :, pl.ds(chunk % 2 * HALF, HALF)],
            store_sem.at[chunk],
        )
        store.start()
        stores.append(store)
    loads[6].wait()
    store = pltpu.make_async_copy(gate, gate_grad.at[0, 0], store_sem.at[6])
    store.start()
    stores.append(store)
    for store in stores:
        store.wait()


def local(queries, keys, values, gates, attended, out_grad, plan, hist_len, block_mask):
    hbm = pl.BlockSpec(memory_space=pl.ANY)
    smem = pl.BlockSpec(memory_space=pltpu.SMEM)
    vmem = pl.BlockSpec(memory_space=pltpu.VMEM)
    out = jax.ShapeDtypeStruct((1, 1, CAP, WIDTH), BF16)
    arrived = jax.ShapeDtypeStruct((6, DP, PACK, QUART), BF16)
    gate_out = jax.ShapeDtypeStruct((CAP, WIDTH), BF16)
    dma = pltpu.SemaphoreType.DMA
    moved, gate_grad = pl.pallas_call(
        kernel,
        out_shape=(arrived, gate_out),
        in_specs=[hbm] * 6 + [smem, smem, vmem],
        out_specs=(hbm,) * 2,
        scratch_shapes=[
            pltpu.VMEM((6, CAP, WIDTH), BF16),
            pltpu.VMEM((8, DP, PACK, QUART), BF16),
            pltpu.VMEM((8, DP, PACK, QUART), BF16),
            pltpu.VMEM((8, 2 * ROWS, QUART), BF16),
            pltpu.VMEM((4, SEQ, ROWS, DH), BF16),
            pltpu.VMEM((NBLK, LEN), F32),
            pltpu.VMEM((LEN, LEN), BF16),
            pltpu.VMEM((LEN, LEN), F32),
            pltpu.VMEM((DH, LEN), BF16),
            pltpu.VMEM((3, SEQ, ROWS, DH), BF16),
            pltpu.VMEM((6, 2, ROWS, QUART), BF16),
            pltpu.VMEM((6, DP, PACK, QUART), BF16),
            pltpu.VMEM((CAP, WIDTH), BF16),
            pltpu.VMEM((2 * ROWS, DP * PACK), BF16),
            pltpu.VMEM((DP * PACK, 2 * ROWS), BF16),
            dma((6,)),
            dma((1,)),
            dma((8,)),
            dma((8,)),
            dma((4,)),
            dma((4,)),
            dma((3,)),
            dma((6,)),
            dma((6,)),
            dma((6,)),
        ],
        compiler_params=pltpu.CompilerParams(
            collective_id=1, has_side_effects=True, vmem_limit_bytes=60 * 2**20
        ),
    )(queries, keys, values, gates, attended, out_grad, plan, hist_len, block_mask)
    return pl.pallas_call(
        unpack,
        out_shape=(out,) * 4,
        in_specs=[hbm] * 2,
        out_specs=(hbm,) * 4,
        scratch_shapes=[
            pltpu.VMEM((6, DP, PACK, QUART), BF16),
            pltpu.VMEM((6, CAP, HALF), BF16),
            pltpu.VMEM((CAP, WIDTH), BF16),
            dma((7,)),
            dma((7,)),
        ],
        compiler_params=pltpu.CompilerParams(vmem_limit_bytes=60 * 2**20),
    )(moved, gate_grad)


def solution(mesh):
    rows = P("dp", "seq", None, None)
    return jax.shard_map(
        local,
        mesh=mesh,
        in_specs=(rows,) * 6 + (P(None, "seq", None), P("dp"), P("dp", None, None)),
        out_specs=(rows,) * 4,
        check_vma=False,
    )
```

```python
import jax
import jax.numpy as jnp
from jax import lax
from jax.experimental import pallas as pl
from jax.experimental.pallas import tpu as pltpu
from jax.sharding import PartitionSpec as P

MESH = pl.DeviceIdType.MESH
F32 = jnp.float32
BF16 = jnp.bfloat16

DP = 16
SEQ = 8
SLOT = 24
CAP = 384
WIDTH = 1024
ROWS = 256
DH = 128
LEN = 2048
NBLK = 16
PACK = 2 * SLOT
HALF = 512
QUART = 256
SCALE = DH ** (-0.5)
TILE = 512
TILES = LEN // TILE

FAR_FIRST = sorted(
    [(i // 4, i % 4) for i in range(1, DP)],
    key=lambda step: -sum(min(i, 4 - i) for i in step),
)

Q, K, G, V = 0, 1, 2, 3
DV, DK, DQ = 0, 1, 2


def kernel(
    queries,
    keys,
    values,
    gates,
    attended,
    out_grad,
    plan,
    hist_len,
    block_mask,
    orecv,
    gate_grad,
    stage,
    dsend,
    drecv,
    comp,
    hist,
    live,
    wt,
    dt,
    key_t,
    grads,
    gath,
    osend,
    gstage,
    place,
    spread,
    load_sem,
    store_sem,
    dsend_sem,
    drecv_sem,
    ssend_sem,
    srecv_sem,
    gsend_sem,
    grecv_sem,
    osend_sem,
    orecv_sem,
):
    dp = lax.axis_index("dp")
    sq = lax.axis_index("seq")
    row_x, row_y = dp // 4, lax.rem(dp, 4)
    zed, core = sq // 2, lax.rem(sq, 2)

    column = [4 * lax.rem(row_x + i, 4) for i in range(4)]
    line = [lax.rem(row_y + i, 4) for i in range(4)]

    barrier = pltpu.get_barrier_semaphore()

    def greet_dp(k, carry):
        pl.semaphore_signal(
            barrier, inc=1, device_id=(lax.rem(dp + k, DP), sq), device_id_type=MESH
        )
        return carry

    def greet_seq(k, carry):
        pl.semaphore_signal(
            barrier, inc=1, device_id=(dp, lax.rem(sq + k, SEQ)), device_id_type=MESH
        )
        return carry

    sources = (queries, keys, attended, gates, out_grad, values)
    loads = [
        pltpu.make_async_copy(src.at[0, 0], stage.at[i], load_sem.at[i])
        for i, src in enumerate(sources)
    ]
    for load in loads:
        load.start()

    lax.fori_loop(1, DP, greet_dp, 0)
    lax.fori_loop(1, SEQ, greet_seq, 0)

    def remote(src, dst, send_sem, recv_sem, target):
        return pltpu.make_async_remote_copy(
            src_ref=src,
            dst_ref=dst,
            send_sem=send_sem,
            recv_sem=recv_sem,
            device_id=target,
            device_id_type=MESH,
        )

    def landed(ref, sem):
        remote(ref, ref, sem, sem, (dp, sq)).wait_recv()

    def left(ref, sem):
        remote(ref, ref, sem, sem, (dp, sq)).wait_send()

    def scatter_dp(src, dst, send_sems, recv_sems, chunk):
        pltpu.make_async_copy(
            src.at[chunk, dp], dst.at[chunk, dp], recv_sems.at[chunk]
        ).start()
        for x, y in FAR_FIRST:
            peer = column[x] + line[y]
            remote(
                src.at[chunk, peer],
                dst.at[chunk, dp],
                send_sems.at[chunk],
                recv_sems.at[chunk],
                (peer, sq),
            ).start()

    def pack_pair(block, array, pair):
        for half in range(2):
            for side in range(2):
                part = block[side * SLOT : (side + 1) * SLOT]
                at = half * HALF
                message = jnp.concatenate(
                    [part[:, at : at + QUART], part[:, at + QUART : at + HALF]], axis=0
                )
                dsend[2 * array + half, 2 * pair + side] = message.astype(BF16)

    def pack(array, slot):
        loads[slot].wait()

        def body(pair, carry):
            at = pl.multiple_of(pair * PACK, PACK)
            pack_pair(stage[slot, pl.ds(at, PACK), :].astype(F32), array, pair)
            return carry

        lax.fori_loop(0, DP // 2, body, 0)

    def send(array, half):
        scatter_dp(dsend, drecv, dsend_sem, drecv_sem, 2 * array + half)

    pack(Q, 0)
    pl.semaphore_wait(barrier, DP - 1 + SEQ - 1)
    send(Q, 0)
    pack(K, 1)
    send(K, 0)

    for i in (2, 3, 4):
        loads[i].wait()
    row48 = lax.broadcasted_iota(jnp.int32, (PACK, 1), 0)

    def norm_body(pair, carry):
        at = pl.multiple_of(pair * PACK, PACK)
        inputs = stage[2, pl.ds(at, PACK), :].astype(F32)
        gate = stage[3, pl.ds(at, PACK), :].astype(F32)
        grad = stage[4, pl.ds(at, PACK), :].astype(F32)
        center = inputs - jnp.mean(inputs, axis=-1, keepdims=True)
        spread_ = jnp.mean(center * center, axis=-1, keepdims=True)
        inv = lax.rsqrt(spread_ + 1e-05)
        normed = center * inv
        first = plan[2 * pair, 0, dp]
        second = plan[2 * pair + 1, 0, dp]
        valid = row48 < jnp.where(row48 < SLOT, first, SLOT + second)
        gstage[pl.ds(at, PACK), :] = jnp.where(valid, grad * normed, 0.0).astype(BF16)
        cot = grad * gate
        mean_cot = jnp.mean(cot, axis=-1, keepdims=True)
        mean_dot = jnp.mean(cot * normed, axis=-1, keepdims=True)
        back = inv * (cot - mean_cot - normed * mean_dot)
        pack_pair(jnp.where(valid, back, 0.0), G, pair)
        return carry

    lax.fori_loop(0, DP // 2, norm_body, 0)
    send(G, 0)
    gate_store = pltpu.make_async_copy(gstage, gate_grad, store_sem.at[0])
    gate_store.start()
    pack(V, 5)

    lane768 = lax.broadcasted_iota(jnp.int32, (1, DP * PACK), 1)
    lane512 = lax.broadcasted_iota(jnp.int32, (1, 2 * ROWS), 1)
    side48 = jnp.where(row48 < SLOT, 0, 1)
    slot48 = row48 - side48 * SLOT

    def target_body(d, carry):
        begin, where_to = carry
        count = plan[dp, 0, d]
        i = lane768 - d * PACK
        side = jnp.where(i < SLOT, 0, 1)
        j = i - side * SLOT
        hit = (i >= 0) & (i < PACK) & (j < count)
        where_to = jnp.where(hit, side * ROWS + begin + j, where_to)
        at = jnp.where(slot48 < count, side48 * ROWS + begin + slot48, -1)
        spread[pl.ds(pl.multiple_of(d * PACK, PACK), PACK), :] = (
            jnp.where(lane512 == at, 1.0, 0.0).astype(BF16)
        )
        return begin + count, where_to

    _, where_to = lax.fori_loop(
        0, DP, target_body, (jnp.int32(0), jnp.full((1, DP * PACK), -1, jnp.int32))
    )

    def place_body(i, carry):
        at = pl.multiple_of(i * 64, 64)
        rows = lax.broadcasted_iota(jnp.int32, (64, 1), 0) + at
        place[pl.ds(at, 64), :] = jnp.where(rows == where_to, 1.0, 0.0).astype(BF16)
        return carry

    lax.fori_loop(0, 2 * ROWS // 64, place_body, 0)

    pattern = block_mask[0].astype(F32)
    block_row = lax.broadcasted_iota(jnp.int32, (NBLK, LEN), 0)
    pos = lax.broadcasted_iota(jnp.int32, (NBLK, LEN), 1)
    onehot = jnp.where(block_row == pos // DH, 1.0, 0.0)
    kept = lax.dot_general(
        pattern, onehot, (((0,), (0,)), ((), ())), preferred_element_type=F32
    )
    length = hist_len[0]
    total = jnp.full((NBLK, LEN), length, jnp.int32).astype(F32)
    inverse = 1.0 / jnp.sqrt(total)
    live[...] = jnp.where(
        ((kept > 0.5) | (onehot > 0.5)) & (pos < length), inverse, 0.0
    )

    def gather_rows(array, half):
        chunk = 2 * array + half
        landed(drecv.at[chunk], drecv_sem.at[chunk])
        block = drecv[chunk].reshape(DP * PACK, QUART)
        comp[chunk] = jnp.dot(place[...], block, preferred_element_type=F32).astype(
            BF16
        )
        for k in range(4):
            to = lax.rem(zed + 2 + k, 4)
            src = comp.at[
                chunk,
                pl.ds(pl.multiple_of(to // 2 * ROWS, ROWS), ROWS),
                pl.ds(pl.multiple_of(lax.rem(to, 2) * DH, DH), DH),
            ]
            dst = hist.at[array, sq]
            peer = 2 * to + half

            @pl.when(sq != peer)
            def _():
                remote(
                    src, dst, ssend_sem.at[array], srecv_sem.at[array], (dp, peer)
                ).start()

            @pl.when(sq == peer)
            def _():
                pltpu.make_async_copy(src, dst, srecv_sem.at[array]).start()

    def history(array):
        landed(hist.at[array], srecv_sem.at[array])

    nt = (((1,), (1,)), ((), ()))

    def tile_rows(array, i):
        return hist[array, pl.ds(2 * i, 2)].reshape(TILE, DH)

    def scores_tile(i, j, diagonal):
        cols = pl.ds(pl.multiple_of(j * TILE, TILE), TILE)
        query = tile_rows(Q, j)
        key = tile_rows(K, i)
        for part in range(TILE // DH):
            base = part * DH
            raw = lax.dot_general(
                key[base : base + DH], query, nt, preferred_element_type=F32
            )
            scores = raw * SCALE
            sig = 0.5 * jnp.tanh(raw * (0.5 * SCALE)) + 0.5
            keep = live[pl.ds(TILE // DH * i + part, 1), cols]
            if diagonal:
                s = lax.broadcasted_iota(jnp.int32, (DH, TILE), 0) + base
                t = lax.broadcasted_iota(jnp.int32, (DH, TILE), 1)
                keep = jnp.where(s <= t, keep, 0.0)
            fac = sig * keep
            weight = scores * fac
            rows = pl.ds(pl.multiple_of(i * TILE + base, DH), DH)
            wt[rows, cols] = weight.astype(BF16)
            dt[rows, cols] = fac + weight * (1.0 - sig)

    def scores_strip(i, carry):
        scores_tile(i, i, True)

        def body(j, c):
            scores_tile(i, j, False)
            return c

        lax.fori_loop(i + 1, TILES, body, 0)
        return carry

    def later_sum(out, array, scale):
        for i in range(TILES):
            acc = jnp.dot(
                wt[i * TILE : (i + 1) * TILE, i * TILE :],
                hist[array, 2 * i :].reshape(LEN - i * TILE, DH),
                preferred_element_type=F32,
            )
            grads[out, 2 * i : 2 * i + 2] = (
                (acc * scale).astype(BF16).reshape(2, ROWS, DH)
            )

    def score_grad_strip(i, carry):
        rows = pl.ds(pl.multiple_of(i * TILE, TILE), TILE)
        value = tile_rows(V, i)

        def body(j, c):
            cols = pl.ds(pl.multiple_of(j * TILE, TILE), TILE)
            products = lax.dot_general(
                value, tile_rows(G, j), nt, preferred_element_type=F32
            )
            wt[rows, cols] = (products * dt[rows, cols]).astype(BF16)
            return c

        lax.fori_loop(i, TILES, body, 0)
        return carry

    def query_sum():
        key_t[...] = hist[K].reshape(LEN, DH).astype(F32).T.astype(BF16)
        for j in range(TILES):
            acc = jnp.dot(
                key_t[:, : (j + 1) * TILE],
                wt[: (j + 1) * TILE, j * TILE : (j + 1) * TILE],
                preferred_element_type=F32,
            )
            grads[DQ, 2 * j : 2 * j + 2] = (
                (acc * SCALE).T.astype(BF16).reshape(2, ROWS, DH)
            )

    def send_grads(out):
        def body(k, carry):
            peer = lax.rem(sq + 4 + k, SEQ)
            src = grads.at[out, peer]
            dst = gath.at[
                2 * out + core,
                zed // 2,
                :,
                pl.ds(pl.multiple_of(lax.rem(zed, 2) * DH, DH), DH),
            ]
            recv_sem = grecv_sem.at[2 * out + core]

            @pl.when(k != 4)
            def _():
                remote(src, dst, gsend_sem.at[out], recv_sem, (dp, peer)).start()

            @pl.when(k == 4)
            def _():
                pltpu.make_async_copy(src, dst, recv_sem).start()

            return carry

        lax.fori_loop(0, SEQ, body, 0)

    def return_rows(out, half):
        chunk = 2 * out + half
        landed(gath.at[chunk], grecv_sem.at[chunk])
        block = gath[chunk].reshape(2 * ROWS, QUART)
        osend[chunk] = (
            jnp.dot(spread[...], block, preferred_element_type=F32)
            .astype(BF16)
            .reshape(DP, PACK, QUART)
        )
        scatter_dp(osend, orecv, osend_sem, orecv_sem, chunk)

    gather_rows(Q, 0)
    send(V, 0)
    gather_rows(K, 0)
    send(Q, 1)
    gather_rows(G, 0)
    send(K, 1)

    @pl.when(core == 0)
    def _():
        history(Q)
        history(K)
        lax.fori_loop(0, 1, scores_strip, 0)

    gather_rows(V, 0)
    send(G, 1)

    @pl.when(core == 0)
    def _():
        lax.fori_loop(1, TILES, scores_strip, 0)
        history(G)
        later_sum(DV, G, 1.0)
        send_grads(DV)

    gather_rows(Q, 1)
    send(V, 1)

    @pl.when(core == 0)
    def _():
        history(V)
        lax.fori_loop(0, TILES, score_grad_strip, 0)

    gather_rows(K, 1)

    @pl.when(core == 0)
    def _():
        later_sum(DK, Q, SCALE)
        send_grads(DK)
        query_sum()
        send_grads(DQ)

    gather_rows(G, 1)

    @pl.when(core == 1)
    def _():
        history(Q)
        history(K)
        lax.fori_loop(0, 1, scores_strip, 0)

    gather_rows(V, 1)
    return_rows(DV, 0)

    @pl.when(core == 1)
    def _():
        lax.fori_loop(1, TILES, scores_strip, 0)

    return_rows(DK, 0)

    @pl.when(core == 1)
    def _():
        history(G)
        later_sum(DV, G, 1.0)
        send_grads(DV)

    return_rows(DQ, 0)

    @pl.when(core == 1)
    def _():
        history(V)
        lax.fori_loop(0, TILES, score_grad_strip, 0)
        later_sum(DK, Q, SCALE)
        send_grads(DK)
        query_sum()
        send_grads(DQ)

    return_rows(DV, 1)
    return_rows(DK, 1)
    return_rows(DQ, 1)

    for chunk in range(8):
        left(dsend.at[chunk, pl.ds(0, DP - 1)], dsend_sem.at[chunk])
    for array in range(4):
        left(hist.at[array, pl.ds(0, SEQ - 1)], ssend_sem.at[array])
    for out in range(3):
        left(grads.at[out, pl.ds(0, SEQ - 1)], gsend_sem.at[out])
    for chunk in range(6):
        landed(orecv.at[chunk], orecv_sem.at[chunk])
        left(osend.at[chunk, pl.ds(0, DP - 1)], osend_sem.at[chunk])
    gate_store.wait()


def unpack(
    moved, gate_in, query_grad, key_grad, value_grad, gate_grad, block, ready, gate, load_sem, store_sem
):
    loads = [
        pltpu.make_async_copy(moved.at[chunk], block.at[chunk], load_sem.at[chunk])
        for chunk in range(6)
    ]
    loads.append(pltpu.make_async_copy(gate_in, gate, load_sem.at[6]))
    for load in loads:
        load.start()
    stores = []
    for chunk in range(6):
        loads[chunk].wait()

        def body(pair, carry):
            at = pl.multiple_of(pair * PACK, PACK)
            one = block[chunk, 2 * pair].astype(F32)
            two = block[chunk, 2 * pair + 1].astype(F32)
            lo = jnp.concatenate([one[:SLOT], two[:SLOT]], axis=0)
            hi = jnp.concatenate([one[SLOT:], two[SLOT:]], axis=0)
            ready[chunk, pl.ds(at, PACK), :QUART] = lo.astype(BF16)
            ready[chunk, pl.ds(at, PACK), QUART:] = hi.astype(BF16)
            return carry

        lax.fori_loop(0, DP // 2, body, 0, unroll=True)
        target = (value_grad, key_grad, query_grad)[chunk // 2]
        store = pltpu.make_async_copy(
            ready.at[chunk],
            target.at[0, 0, :, pl.ds(chunk % 2 * HALF, HALF)],
            store_sem.at[chunk],
        )
        store.start()
        stores.append(store)
    loads[6].wait()
    store = pltpu.make_async_copy(gate, gate_grad.at[0, 0], store_sem.at[6])
    store.start()
    stores.append(store)
    for store in stores:
        store.wait()


def local(queries, keys, values, gates, attended, out_grad, plan, hist_len, block_mask):
    hbm = pl.BlockSpec(memory_space=pl.ANY)
    smem = pl.BlockSpec(memory_space=pltpu.SMEM)
    vmem = pl.BlockSpec(memory_space=pltpu.VMEM)
    out = jax.ShapeDtypeStruct((1, 1, CAP, WIDTH), BF16)
    arrived = jax.ShapeDtypeStruct((6, DP, PACK, QUART), BF16)
    gate_out = jax.ShapeDtypeStruct((CAP, WIDTH), BF16)
    dma = pltpu.SemaphoreType.DMA
    moved, gate_grad = pl.pallas_call(
        kernel,
        out_shape=(arrived, gate_out),
        in_specs=[hbm] * 6 + [smem, smem, vmem],
        out_specs=(hbm,) * 2,
        scratch_shapes=[
            pltpu.VMEM((6, CAP, WIDTH), BF16),
            pltpu.VMEM((8, DP, PACK, QUART), BF16),
            pltpu.VMEM((8, DP, PACK, QUART), BF16),
            pltpu.VMEM((8, 2 * ROWS, QUART), BF16),
            pltpu.VMEM((4, SEQ, ROWS, DH), BF16),
            pltpu.VMEM((NBLK, LEN), F32),
            pltpu.VMEM((LEN, LEN), BF16),
            pltpu.VMEM((LEN, LEN), F32),
            pltpu.VMEM((DH, LEN), BF16),
            pltpu.VMEM((3, SEQ, ROWS, DH), BF16),
            pltpu.VMEM((6, 2, ROWS, QUART), BF16),
            pltpu.VMEM((6, DP, PACK, QUART), BF16),
            pltpu.VMEM((CAP, WIDTH), BF16),
            pltpu.VMEM((2 * ROWS, DP * PACK), BF16),
            pltpu.VMEM((DP * PACK, 2 * ROWS), BF16),
            dma((6,)),
            dma((1,)),
            dma((8,)),
            dma((8,)),
            dma((4,)),
            dma((4,)),
            dma((3,)),
            dma((6,)),
            dma((6,)),
            dma((6,)),
        ],
        compiler_params=pltpu.CompilerParams(
            collective_id=1, has_side_effects=True, vmem_limit_bytes=60 * 2**20
        ),
    )(queries, keys, values, gates, attended, out_grad, plan, hist_len, block_mask)
    return pl.pallas_call(
        unpack,
        out_shape=(out,) * 4,
        in_specs=[hbm] * 2,
        out_specs=(hbm,) * 4,
        scratch_shapes=[
            pltpu.VMEM((6, DP, PACK, QUART), BF16),
            pltpu.VMEM((6, CAP, HALF), BF16),
            pltpu.VMEM((CAP, WIDTH), BF16),
            dma((7,)),
            dma((7,)),
        ],
        compiler_params=pltpu.CompilerParams(vmem_limit_bytes=60 * 2**20),
    )(moved, gate_grad)


def solution(mesh):
    rows = P("dp", "seq", None, None)
    return jax.shard_map(
        local,
        mesh=mesh,
        in_specs=(rows,) * 6 + (P(None, "seq", None), P("dp"), P("dp", None, None)),
        out_specs=(rows,) * 4,
        check_vma=False,
    )
```

```python
import jax
import jax.numpy as jnp
from jax import lax
from jax.experimental import pallas as pl
from jax.experimental.pallas import tpu as pltpu
from jax.sharding import PartitionSpec as P

MESH = pl.DeviceIdType.MESH
F32 = jnp.float32
BF16 = jnp.bfloat16

DP = 16
SEQ = 8
SLOT = 24
CAP = 384
WIDTH = 1024
ROWS = 256
DH = 128
LEN = 2048
NBLK = 16
PACK = 2 * SLOT
HALF = 512
QUART = 256
SCALE = DH ** (-0.5)
TILE = 512
TILES = LEN // TILE

FAR_FIRST = sorted(
    [(i // 4, i % 4) for i in range(1, DP)],
    key=lambda step: -sum(min(i, 4 - i) for i in step),
)

Q, K, G, V = 0, 1, 2, 3
DV, DK, DQ = 0, 1, 2


def kernel(
    queries,
    keys,
    values,
    gates,
    attended,
    out_grad,
    plan,
    hist_len,
    block_mask,
    orecv,
    gate_grad,
    stage,
    dsend,
    drecv,
    comp,
    hist,
    live,
    wt,
    dt,
    key_t,
    grads,
    gath,
    osend,
    gstage,
    place,
    spread,
    load_sem,
    store_sem,
    dsend_sem,
    drecv_sem,
    ssend_sem,
    srecv_sem,
    gsend_sem,
    grecv_sem,
    osend_sem,
    orecv_sem,
):
    dp = lax.axis_index("dp")
    sq = lax.axis_index("seq")
    row_x, row_y = dp // 4, lax.rem(dp, 4)
    zed, core = sq // 2, lax.rem(sq, 2)

    column = [4 * lax.rem(row_x + i, 4) for i in range(4)]
    line = [lax.rem(row_y + i, 4) for i in range(4)]

    barrier = pltpu.get_barrier_semaphore()

    def greet_dp(k, carry):
        pl.semaphore_signal(
            barrier, inc=1, device_id=(lax.rem(dp + k, DP), sq), device_id_type=MESH
        )
        return carry

    def greet_seq(k, carry):
        pl.semaphore_signal(
            barrier, inc=1, device_id=(dp, lax.rem(sq + k, SEQ)), device_id_type=MESH
        )
        return carry

    sources = (queries, keys, attended, gates, out_grad, values)
    loads = [
        pltpu.make_async_copy(src.at[0, 0], stage.at[i], load_sem.at[i])
        for i, src in enumerate(sources)
    ]
    for load in loads:
        load.start()

    lax.fori_loop(1, DP, greet_dp, 0)
    lax.fori_loop(1, SEQ, greet_seq, 0)

    def remote(src, dst, send_sem, recv_sem, target):
        return pltpu.make_async_remote_copy(
            src_ref=src,
            dst_ref=dst,
            send_sem=send_sem,
            recv_sem=recv_sem,
            device_id=target,
            device_id_type=MESH,
        )

    def landed(ref, sem):
        remote(ref, ref, sem, sem, (dp, sq)).wait_recv()

    def left(ref, sem):
        remote(ref, ref, sem, sem, (dp, sq)).wait_send()

    def scatter_dp(src, dst, send_sems, recv_sems, chunk):
        pltpu.make_async_copy(
            src.at[chunk, dp], dst.at[chunk, dp], recv_sems.at[chunk]
        ).start()
        for x, y in FAR_FIRST:
            peer = column[x] + line[y]
            remote(
                src.at[chunk, peer],
                dst.at[chunk, dp],
                send_sems.at[chunk],
                recv_sems.at[chunk],
                (peer, sq),
            ).start()

    def pack_pair(block, array, pair, halves=(0, 1)):
        for half in halves:
            for side in range(2):
                part = block[side * SLOT : (side + 1) * SLOT]
                at = half * HALF
                message = jnp.concatenate(
                    [part[:, at : at + QUART], part[:, at + QUART : at + HALF]], axis=0
                )
                dsend[2 * array + half, 2 * pair + side] = message.astype(BF16)

    def pack(array, slot, halves=(0, 1)):
        def body(pair, carry):
            at = pl.multiple_of(pair * PACK, PACK)
            block = stage[slot, pl.ds(at, PACK), :].astype(F32)
            pack_pair(block, array, pair, halves)
            return carry

        lax.fori_loop(0, DP // 2, body, 0)

    def send(array, half):
        scatter_dp(dsend, drecv, dsend_sem, drecv_sem, 2 * array + half)

    loads[0].wait()
    pack(Q, 0, (0,))
    pl.semaphore_wait(barrier, DP - 1 + SEQ - 1)
    send(Q, 0)
    loads[1].wait()
    pack(K, 1, (0,))
    send(K, 0)
    pack(Q, 0, (1,))
    pack(K, 1, (1,))

    for i in (2, 3, 4):
        loads[i].wait()
    row48 = lax.broadcasted_iota(jnp.int32, (PACK, 1), 0)

    def norm_body(pair, carry):
        at = pl.multiple_of(pair * PACK, PACK)
        inputs = stage[2, pl.ds(at, PACK), :].astype(F32)
        gate = stage[3, pl.ds(at, PACK), :].astype(F32)
        grad = stage[4, pl.ds(at, PACK), :].astype(F32)
        center = inputs - jnp.mean(inputs, axis=-1, keepdims=True)
        spread_ = jnp.mean(center * center, axis=-1, keepdims=True)
        inv = lax.rsqrt(spread_ + 1e-05)
        normed = center * inv
        first = plan[2 * pair, 0, dp]
        second = plan[2 * pair + 1, 0, dp]
        valid = row48 < jnp.where(row48 < SLOT, first, SLOT + second)
        gstage[pl.ds(at, PACK), :] = jnp.where(valid, grad * normed, 0.0).astype(BF16)
        cot = grad * gate
        mean_cot = jnp.mean(cot, axis=-1, keepdims=True)
        mean_dot = jnp.mean(cot * normed, axis=-1, keepdims=True)
        back = inv * (cot - mean_cot - normed * mean_dot)
        pack_pair(jnp.where(valid, back, 0.0), G, pair)
        return carry

    lax.fori_loop(0, DP // 2, norm_body, 0)
    send(G, 0)
    gate_store = pltpu.make_async_copy(gstage, gate_grad, store_sem.at[0])
    gate_store.start()
    loads[5].wait()
    pack(V, 5)

    lane768 = lax.broadcasted_iota(jnp.int32, (1, DP * PACK), 1)
    lane512 = lax.broadcasted_iota(jnp.int32, (1, 2 * ROWS), 1)
    side48 = jnp.where(row48 < SLOT, 0, 1)
    slot48 = row48 - side48 * SLOT

    def target_body(d, carry):
        begin, where_to = carry
        count = plan[dp, 0, d]
        i = lane768 - d * PACK
        side = jnp.where(i < SLOT, 0, 1)
        j = i - side * SLOT
        hit = (i >= 0) & (i < PACK) & (j < count)
        where_to = jnp.where(hit, side * ROWS + begin + j, where_to)
        at = jnp.where(slot48 < count, side48 * ROWS + begin + slot48, -1)
        spread[pl.ds(pl.multiple_of(d * PACK, PACK), PACK), :] = (
            jnp.where(lane512 == at, 1.0, 0.0).astype(BF16)
        )
        return begin + count, where_to

    _, where_to = lax.fori_loop(
        0, DP, target_body, (jnp.int32(0), jnp.full((1, DP * PACK), -1, jnp.int32))
    )

    def place_body(i, carry):
        at = pl.multiple_of(i * 64, 64)
        rows = lax.broadcasted_iota(jnp.int32, (64, 1), 0) + at
        place[pl.ds(at, 64), :] = jnp.where(rows == where_to, 1.0, 0.0).astype(BF16)
        return carry

    lax.fori_loop(0, 2 * ROWS // 64, place_body, 0)

    pattern = block_mask[0].astype(F32)
    block_row = lax.broadcasted_iota(jnp.int32, (NBLK, LEN), 0)
    pos = lax.broadcasted_iota(jnp.int32, (NBLK, LEN), 1)
    onehot = jnp.where(block_row == pos // DH, 1.0, 0.0)
    kept = lax.dot_general(
        pattern, onehot, (((0,), (0,)), ((), ())), preferred_element_type=F32
    )
    length = hist_len[0]
    total = jnp.full((NBLK, LEN), length, jnp.int32).astype(F32)
    inverse = 1.0 / jnp.sqrt(total)
    live[...] = jnp.where(
        ((kept > 0.5) | (onehot > 0.5)) & (pos < length), inverse, 0.0
    )

    def gather_rows(array, half):
        chunk = 2 * array + half
        landed(drecv.at[chunk], drecv_sem.at[chunk])
        block = drecv[chunk].reshape(DP * PACK, QUART)
        comp[chunk] = jnp.dot(place[...], block, preferred_element_type=F32).astype(
            BF16
        )
        for k in range(4):
            to = lax.rem(zed + 2 + k, 4)
            src = comp.at[
                chunk,
                pl.ds(pl.multiple_of(to // 2 * ROWS, ROWS), ROWS),
                pl.ds(pl.multiple_of(lax.rem(to, 2) * DH, DH), DH),
            ]
            dst = hist.at[array, sq]
            peer = 2 * to + half

            @pl.when(sq != peer)
            def _():
                remote(
                    src, dst, ssend_sem.at[array], srecv_sem.at[array], (dp, peer)
                ).start()

            @pl.when(sq == peer)
            def _():
                pltpu.make_async_copy(src, dst, srecv_sem.at[array]).start()

    def history(array):
        landed(hist.at[array], srecv_sem.at[array])

    nt = (((1,), (1,)), ((), ()))

    def tile_rows(array, i):
        return hist[array, pl.ds(2 * i, 2)].reshape(TILE, DH)

    def scores_tile(i, j, diagonal):
        cols = pl.ds(pl.multiple_of(j * TILE, TILE), TILE)
        query = tile_rows(Q, j)
        key = tile_rows(K, i)
        for part in range(TILE // DH):
            base = part * DH
            raw = lax.dot_general(
                key[base : base + DH], query, nt, preferred_element_type=F32
            )
            scores = raw * SCALE
            sig = 0.5 * jnp.tanh(raw * (0.5 * SCALE)) + 0.5
            keep = live[pl.ds(TILE // DH * i + part, 1), cols]
            if diagonal:
                s = lax.broadcasted_iota(jnp.int32, (DH, TILE), 0) + base
                t = lax.broadcasted_iota(jnp.int32, (DH, TILE), 1)
                keep = jnp.where(s <= t, keep, 0.0)
            fac = sig * keep
            weight = scores * fac
            rows = pl.ds(pl.multiple_of(i * TILE + base, DH), DH)
            wt[rows, cols] = weight.astype(BF16)
            dt[rows, cols] = fac + weight * (1.0 - sig)

    def scores_strip(i, carry):
        scores_tile(i, i, True)

        def body(j, c):
            scores_tile(i, j, False)
            return c

        lax.fori_loop(i + 1, TILES, body, 0)
        return carry

    def later_sum(out, array, scale):
        for i in range(TILES):
            acc = jnp.dot(
                wt[i * TILE : (i + 1) * TILE, i * TILE :],
                hist[array, 2 * i :].reshape(LEN - i * TILE, DH),
                preferred_element_type=F32,
            )
            grads[out, 2 * i : 2 * i + 2] = (
                (acc * scale).astype(BF16).reshape(2, ROWS, DH)
            )

    def score_grad_strip(i, carry):
        rows = pl.ds(pl.multiple_of(i * TILE, TILE), TILE)
        value = tile_rows(V, i)

        def body(j, c):
            cols = pl.ds(pl.multiple_of(j * TILE, TILE), TILE)
            products = lax.dot_general(
                value, tile_rows(G, j), nt, preferred_element_type=F32
            )
            wt[rows, cols] = (products * dt[rows, cols]).astype(BF16)
            return c

        lax.fori_loop(i, TILES, body, 0)
        return carry

    def query_sum():
        key_t[...] = hist[K].reshape(LEN, DH).astype(F32).T.astype(BF16)
        for j in range(TILES):
            acc = jnp.dot(
                key_t[:, : (j + 1) * TILE],
                wt[: (j + 1) * TILE, j * TILE : (j + 1) * TILE],
                preferred_element_type=F32,
            )
            grads[DQ, 2 * j : 2 * j + 2] = (
                (acc * SCALE).T.astype(BF16).reshape(2, ROWS, DH)
            )

    def send_grads(out):
        def body(k, carry):
            peer = lax.rem(sq + 4 + k, SEQ)
            src = grads.at[out, peer]
            dst = gath.at[
                2 * out + core,
                zed // 2,
                :,
                pl.ds(pl.multiple_of(lax.rem(zed, 2) * DH, DH), DH),
            ]
            recv_sem = grecv_sem.at[2 * out + core]

            @pl.when(k != 4)
            def _():
                remote(src, dst, gsend_sem.at[out], recv_sem, (dp, peer)).start()

            @pl.when(k == 4)
            def _():
                pltpu.make_async_copy(src, dst, recv_sem).start()

            return carry

        lax.fori_loop(0, SEQ, body, 0)

    def return_rows(out, half):
        chunk = 2 * out + half
        landed(gath.at[chunk], grecv_sem.at[chunk])
        block = gath[chunk].reshape(2 * ROWS, QUART)
        osend[chunk] = (
            jnp.dot(spread[...], block, preferred_element_type=F32)
            .astype(BF16)
            .reshape(DP, PACK, QUART)
        )
        scatter_dp(osend, orecv, osend_sem, orecv_sem, chunk)

    gather_rows(Q, 0)
    send(V, 0)
    gather_rows(K, 0)
    send(Q, 1)
    gather_rows(G, 0)
    send(K, 1)

    @pl.when(core == 0)
    def _():
        history(Q)
        history(K)
        lax.fori_loop(0, 1, scores_strip, 0)

    gather_rows(V, 0)
    send(G, 1)

    @pl.when(core == 0)
    def _():
        lax.fori_loop(1, TILES, scores_strip, 0)
        history(G)
        later_sum(DV, G, 1.0)
        send_grads(DV)

    gather_rows(Q, 1)
    send(V, 1)

    @pl.when(core == 0)
    def _():
        history(V)
        lax.fori_loop(0, TILES, score_grad_strip, 0)

    gather_rows(K, 1)

    @pl.when(core == 0)
    def _():
        later_sum(DK, Q, SCALE)
        send_grads(DK)
        query_sum()
        send_grads(DQ)

    gather_rows(G, 1)

    @pl.when(core == 1)
    def _():
        history(Q)
        history(K)
        lax.fori_loop(0, 1, scores_strip, 0)

    gather_rows(V, 1)
    return_rows(DV, 0)

    @pl.when(core == 1)
    def _():
        lax.fori_loop(1, TILES, scores_strip, 0)

    return_rows(DK, 0)

    @pl.when(core == 1)
    def _():
        history(G)
        later_sum(DV, G, 1.0)
        send_grads(DV)
        history(V)
        lax.fori_loop(0, TILES, score_grad_strip, 0)

    return_rows(DQ, 0)

    @pl.when(core == 1)
    def _():
        later_sum(DK, Q, SCALE)
        send_grads(DK)
        query_sum()
        send_grads(DQ)

    return_rows(DV, 1)
    return_rows(DK, 1)
    return_rows(DQ, 1)

    for chunk in range(8):
        left(dsend.at[chunk, pl.ds(0, DP - 1)], dsend_sem.at[chunk])
    for array in range(4):
        left(hist.at[array, pl.ds(0, SEQ - 1)], ssend_sem.at[array])
    for out in range(3):
        left(grads.at[out, pl.ds(0, SEQ - 1)], gsend_sem.at[out])
    for chunk in range(6):
        landed(orecv.at[chunk], orecv_sem.at[chunk])
        left(osend.at[chunk, pl.ds(0, DP - 1)], osend_sem.at[chunk])
    gate_store.wait()


def unpack(
    moved, gate_in, query_grad, key_grad, value_grad, gate_grad, block, ready, gate, load_sem, store_sem
):
    loads = [
        pltpu.make_async_copy(moved.at[chunk], block.at[chunk], load_sem.at[chunk])
        for chunk in range(6)
    ]
    loads.append(pltpu.make_async_copy(gate_in, gate, load_sem.at[6]))
    for load in loads:
        load.start()
    stores = []
    for chunk in range(6):
        loads[chunk].wait()

        def body(pair, carry):
            at = pl.multiple_of(pair * PACK, PACK)
            one = block[chunk, 2 * pair].astype(F32)
            two = block[chunk, 2 * pair + 1].astype(F32)
            lo = jnp.concatenate([one[:SLOT], two[:SLOT]], axis=0)
            hi = jnp.concatenate([one[SLOT:], two[SLOT:]], axis=0)
            ready[chunk, pl.ds(at, PACK), :QUART] = lo.astype(BF16)
            ready[chunk, pl.ds(at, PACK), QUART:] = hi.astype(BF16)
            return carry

        lax.fori_loop(0, DP // 2, body, 0, unroll=True)
        target = (value_grad, key_grad, query_grad)[chunk // 2]
        store = pltpu.make_async_copy(
            ready.at[chunk],
            target.at[0, 0, :, pl.ds(chunk % 2 * HALF, HALF)],
            store_sem.at[chunk],
        )
        store.start()
        stores.append(store)
    loads[6].wait()
    store = pltpu.make_async_copy(gate, gate_grad.at[0, 0], store_sem.at[6])
    store.start()
    stores.append(store)
    for store in stores:
        store.wait()


def local(queries, keys, values, gates, attended, out_grad, plan, hist_len, block_mask):
    hbm = pl.BlockSpec(memory_space=pl.ANY)
    smem = pl.BlockSpec(memory_space=pltpu.SMEM)
    vmem = pl.BlockSpec(memory_space=pltpu.VMEM)
    out = jax.ShapeDtypeStruct((1, 1, CAP, WIDTH), BF16)
    arrived = jax.ShapeDtypeStruct((6, DP, PACK, QUART), BF16)
    gate_out = jax.ShapeDtypeStruct((CAP, WIDTH), BF16)
    dma = pltpu.SemaphoreType.DMA
    moved, gate_grad = pl.pallas_call(
        kernel,
        out_shape=(arrived, gate_out),
        in_specs=[hbm] * 6 + [smem, smem, vmem],
        out_specs=(hbm,) * 2,
        scratch_shapes=[
            pltpu.VMEM((6, CAP, WIDTH), BF16),
            pltpu.VMEM((8, DP, PACK, QUART), BF16),
            pltpu.VMEM((8, DP, PACK, QUART), BF16),
            pltpu.VMEM((8, 2 * ROWS, QUART), BF16),
            pltpu.VMEM((4, SEQ, ROWS, DH), BF16),
            pltpu.VMEM((NBLK, LEN), F32),
            pltpu.VMEM((LEN, LEN), BF16),
            pltpu.VMEM((LEN, LEN), F32),
            pltpu.VMEM((DH, LEN), BF16),
            pltpu.VMEM((3, SEQ, ROWS, DH), BF16),
            pltpu.VMEM((6, 2, ROWS, QUART), BF16),
            pltpu.VMEM((6, DP, PACK, QUART), BF16),
            pltpu.VMEM((CAP, WIDTH), BF16),
            pltpu.VMEM((2 * ROWS, DP * PACK), BF16),
            pltpu.VMEM((DP * PACK, 2 * ROWS), BF16),
            dma((6,)),
            dma((1,)),
            dma((8,)),
            dma((8,)),
            dma((4,)),
            dma((4,)),
            dma((3,)),
            dma((6,)),
            dma((6,)),
            dma((6,)),
        ],
        compiler_params=pltpu.CompilerParams(
            collective_id=1, has_side_effects=True, vmem_limit_bytes=60 * 2**20
        ),
    )(queries, keys, values, gates, attended, out_grad, plan, hist_len, block_mask)
    return pl.pallas_call(
        unpack,
        out_shape=(out,) * 4,
        in_specs=[hbm] * 2,
        out_specs=(hbm,) * 4,
        scratch_shapes=[
            pltpu.VMEM((6, DP, PACK, QUART), BF16),
            pltpu.VMEM((6, CAP, HALF), BF16),
            pltpu.VMEM((CAP, WIDTH), BF16),
            dma((7,)),
            dma((7,)),
        ],
        compiler_params=pltpu.CompilerParams(vmem_limit_bytes=60 * 2**20),
    )(moved, gate_grad)


def solution(mesh):
    rows = P("dp", "seq", None, None)
    return jax.shard_map(
        local,
        mesh=mesh,
        in_specs=(rows,) * 6 + (P(None, "seq", None), P("dp"), P("dp", None, None)),
        out_specs=(rows,) * 4,
        check_vma=False,
    )
```
